32 devices in a mesh: groups: 2 (over x), req: 8 (over z, y), tp: 2 (over core).
Axes of the slice: x: 2, y: 2, z: 4, core: 2. Of those that a mesh axis runs over, the one named last changes fastest.
Arguments:
- x_inputs: bfloat16 [32, 256, 4096], P(('groups', 'req'), None, 'tp'), parts along dimension 0, may hold values from -6 to 6
- z_gates: bfloat16 [32, 256, 4096], P(('groups', 'req'), None, 'tp'), parts along dimension 0, may hold values from -6 to 6
- b_proj: bfloat16 [32, 256, 256], P(('groups', 'req')), parts along dimension 0, may hold values from -1.5 to 1.5
- c_proj: bfloat16 [32, 256, 256], P(('groups', 'req')), parts along dimension 0, may hold values from -1.5 to 1.5
- dt_raw: float32 [32, 256, 32], P(('groups', 'req'), None, 'tp'), parts along dimension 0, may hold values from -1.5 to 7.5
- dt_bias: float32 [32], P('tp'), may hold values from -4.5 to -3.8
- a_log: float32 [32], P('tp'), may hold values from -2.31 to 2.08
- d_skip: float32 [32], P('tp'), may hold values from 0.5 to 1.5
- pool_codes: bfloat16 [2048, 64, 256], P(('groups', 'req', 'tp')), parts along dimension 0, may hold values from -6 to 6
- pool_scales: bfloat16 [2048, 64], P(('groups', 'req', 'tp')), parts along dimension 0, may hold values from 0.049804688 to 0.5
- page_holder: int32 [2, 32, 32, 1], P('tp', 'groups'), parts along dimension 1, may hold values from 0 to 7; in each aligned block of 64 rows (0 to 63, 64 to 127, ..., all dimensions but the last counted through in order) at most 16 rows name the same one
- page_index: int32 [2, 32, 32], P('tp', 'groups'), parts along dimension 1, may hold values from 0 to 63
- hit_blocks: int32 [32], P(('groups', 'req')), parts along dimension 0, may hold values 0 or 1
- suffix_len: int32 [32], P(('groups', 'req')), parts along dimension 0, may hold values from 1 to 256, 3072 in all
- w_out: bfloat16 [4096, 2, 2560], P(None, 'tp', 'req'), may hold values from -0.09375 to 0.09375
Outputs:
- mixed_out: bfloat16 [32, 256, 5120], P(('groups', 'req'), None, 'tp'), parts along dimension 0
- end_state: bfloat16 [32, 4096, 256], P(('groups', 'req'), 'tp'), parts along dimension 0
The draws below stay inside these ranges and needn't reach their ends.
There are 2 independent parts, one for each index of `groups`. The reference program is written for one: setup_inputs(seed, part) draws one part's arguments, and reference() takes and returns one part's arrays. A program takes and returns all parts, laid end to end along the dimension named above; an argument that names none is the same for every part. Nothing has to cross between parts.
Inputs may be any that keep to these rules, and one draw needn't show every extreme that they name: `page_holder`: in each aligned block of 64 rows (the pages of one device's requests on one tp index) no holder is named more than 16 times, a bound that some block reaches. `suffix_len`: some request has 256 suffix tokens.
All inputs are finite; a program needn't handle non-finite values. No bound on the sum of `hit_blocks` or of `suffix_len` on one device may be relied on, other than what follows from the above.
Results may differ from the reference program's by a relative error of at most 0.0055.
Values may be sent and summed in bfloat16 or wider, within the bound.
No kernel may reach another device: no remote copies, remote signals or barrier semaphores. Data moves between devices by JAX's collectives and lax.ppermute only.
A program may use at most 128 MiB of HBM per device.

```python
import math
import jax
import jax.numpy as jnp
import numpy as np
from jax import lax

D = 5120
HD = 128
STATE = 256
HEADS = 32
SUFFIX_SLOTS = 256
R_DEV = 2
POOL = 64
PROWS = 64
INNER = 4096
REQUEST_COUNT = 16
PAGES_TP = 32
CAP = 16
POOLS = 1024
N_REQ = 8
N_TP = 2


def draw_a_log(key, part):
    key = jax.random.fold_in(key, 11)
    key_fast, key_slow, key_quick = jax.random.split(key, 3)
    fast_share = 0.5
    fast_mask = jax.random.uniform(key_fast, (HEADS,)) < fast_share
    slow_rate = jnp.exp(jax.random.uniform(key_slow, (HEADS,), minval=math.log(0.1), maxval=math.log(0.2)))
    quick_rate = jnp.exp(jax.random.uniform(key_quick, (HEADS,), minval=math.log(3.0), maxval=math.log(8.0)))
    return jnp.log(jnp.where(fast_mask, quick_rate, slow_rate)).astype(jnp.float32)


def draw_dt_raw(key, part):
    key = jax.random.fold_in(key, 12)
    key_base, key_positions = jax.random.split(key)
    starting_values = jnp.clip(0.5 * jax.random.normal(key_base, (REQUEST_COUNT, SUFFIX_SLOTS, HEADS)), -1.5, 1.5)
    spike_positions = jax.random.randint(key_positions, (REQUEST_COUNT, 2), 0, SUFFIX_SLOTS)
    spike_mask = jnp.any(jnp.arange(SUFFIX_SLOTS)[None, :, None] == spike_positions[:, None, :], axis=2)
    return (starting_values + 6.0 * spike_mask[:, :, None].astype(jnp.float32)).astype(jnp.float32)


def set_ends(values, rng, least, largest):
    extent = values.shape
    place = [jax.random.randint(jax.random.fold_in(rng, axis), (), 0, extent[axis]) for axis in range(len(extent))]
    values = values.at[tuple(place)].set(least)
    longest = extent.index(max(extent))
    place[longest] = (place[longest] + 1) % extent[longest]
    return values.at[tuple(place)].set(largest)


def levels(stream_key, dims, shards, least, high):
    def one(axis_at, parts):
        steps = jax.random.uniform(jax.random.fold_in(jax.random.fold_in(stream_key, 6), axis_at), (parts,), jnp.float32, least / len(shards), high / len(shards))
        return jnp.repeat(jnp.exp(steps), dims[axis_at] // parts).reshape((-1,) + (1,) * (len(dims) - axis_at - 1))

    factor_of = one(*shards[0])
    for cut in shards[1:]:
        factor_of = factor_of * one(*cut)
    return factor_of


def length_profile(amount, total, most, skew):
    weights = [(1 << 20) // math.isqrt(standing ** skew) + 1 for standing in range(2, amount + 1)]
    rest, given = total - most - (amount - 1), [1] * (amount - 1)
    while rest > 0:
        candidates = [i for i in range(amount - 1) if given[i] < most]
        whole, budget = sum([weights[i] for i in candidates]), rest
        for i in candidates:
            extra = min(most - given[i], max(1, budget * weights[i] // whole), rest)
            given[i] = given[i] + extra
            rest = rest - extra
    return np.array([most] + given)


def ragged(rng, number_of, total, bound, slope):
    if number_of == 2:
        one = jax.random.randint(rng, (), max(1, total - bound), min(bound, total - 1) + 1)
        return jnp.stack([one, total - one])
    lengths = jnp.asarray(length_profile(number_of, total, bound, slope), jnp.int32)
    twos = (number_of - 1) // 2
    giver, taker = lengths[1:1 + 2 * twos:2], lengths[2:2 + 2 * twos:2]
    slack = jnp.minimum(giver - 1, bound - taker)
    passed = jax.random.randint(jax.random.fold_in(rng, 1), (twos,), 0, 1 << 20) % (slack + 1)
    lengths = lengths.at[1:1 + 2 * twos:2].set(giver - passed).at[2:2 + 2 * twos:2].set(taker + passed)
    return lengths[jax.random.permutation(jax.random.fold_in(rng, 2), number_of)]


def routed_block(own_key, own, number, rows, count, top, limit, slope):
    order = jax.random.permutation(own_key, count)
    crowded, ordinary = load_shares(count, rows * top, limit, slope, True), load_shares(count, rows * top, limit, slope, False)
    places = jnp.arange(count)

    def named(sizes, turn):
        used = int((sizes > 0).sum())
        fixed = max(1, used // 4)
        shifted = fixed + (places - fixed + turn * (used - fixed)) % max(1, count - fixed)
        return jnp.zeros((count,), jnp.int32).at[order[jnp.where(places < fixed, places, shifted)]].set(jnp.asarray(sizes, jnp.int32))

    sizes = jnp.where(number % 4 == 0, named(crowded, number // 4), named(ordinary, number - number // 4 - 1))
    mixed = jax.random.permutation(jax.random.fold_in(own, 3), count)
    giver, sink = mixed[0:count // 2 * 2:2], mixed[1:count // 2 * 2:2]
    slack = jnp.minimum(sizes[giver] - 1, limit - sizes[sink]) // 2
    slack = jnp.where((giver == order[0]) | (sink == order[0]) | (sizes[sink] == 0), 0, jnp.maximum(slack, 0))
    shifted = jax.random.randint(jax.random.fold_in(own, 4), (count // 2,), 0, 1 << 20) % (slack + 1)
    sizes = sizes.at[giver].add(-shifted).at[sink].add(shifted)
    labels = jnp.searchsorted(jnp.cumsum(sizes), jnp.arange(rows * top), side="right").astype(jnp.int32)
    grid = labels.reshape(top, rows).T
    grid = grid[jax.random.permutation(jax.random.fold_in(own, 1), rows)]
    turn = jax.random.randint(jax.random.fold_in(own, 2), (rows, 1), 0, top)
    return jnp.take_along_axis(grid, (jnp.arange(top)[None, :] + turn) % top, axis=1)


def load_shares(number_of, total, most, skew, full):
    portions = [(1 << 20) // math.isqrt(rank ** skew) + 1 for rank in range(1, number_of + 1)]
    largest = most if full else min(most, max(-(-total // number_of), total * portions[0] // sum(portions)))
    least = 1 if total - largest >= number_of - 1 else 0
    counts, surplus = [largest] + [least] * (number_of - 1), total - largest - least * (number_of - 1)
    while surplus > 0:
        candidates = [i for i in range(1, number_of) if counts[i] < largest] or [i for i in range(1, number_of) if counts[i] < most]
        whole, remaining = sum([portions[i] for i in candidates]), surplus
        for i in candidates:
            more = min(most - counts[i], max(1, remaining * portions[i] // whole), surplus)
            counts[i] = counts[i] + more
            surplus = surplus - more
    return np.array(counts)


def scatter_about(key, extent, deviation, limit, cuts=(), held_as=jnp.bfloat16):
    drawn = jax.random.normal(key, extent, jnp.float32) * deviation
    if len(cuts) > 0:
        drawn = levels(key, extent, cuts, -0.22, 0.18) * drawn
    return jnp.clip(drawn, min=-limit, max=limit).astype(held_as)


def setup_inputs(seed: int = 0, part: int = 0) -> dict:
    seeds = jax.random.split(jax.random.key(seed), 16)
    part_splits = jax.random.split(jax.random.fold_in(seeds[15], part), 16)
    x_inputs = scatter_about(part_splits[0], (REQUEST_COUNT, SUFFIX_SLOTS, INNER), 1.0, 6.0, ((0, 8), (2, 2)))
    z_gates = scatter_about(part_splits[1], (REQUEST_COUNT, SUFFIX_SLOTS, INNER), 1.0, 6.0, ((0, 8), (2, 2)))
    b_proj = scatter_about(part_splits[2], (REQUEST_COUNT, SUFFIX_SLOTS, STATE), 0.25, 1.5, ((0, 8),))
    c_proj = scatter_about(part_splits[3], (REQUEST_COUNT, SUFFIX_SLOTS, STATE), 0.25, 1.5, ((0, 8),))
    dt_raw = draw_dt_raw(jax.random.fold_in(jax.random.fold_in(seeds[15], part), 71), part)
    dt_bias = jnp.clip(-4.5 + 0.70000005 * jax.random.uniform(seeds[5], (HEADS,), jnp.float32) ** levels(seeds[5], (HEADS,), ((0, 2),), -0.2, 0.2), -4.5, -3.8)
    a_log = draw_a_log(jax.random.fold_in(seeds[15], 71), part)
    d_skip = jnp.clip(0.5 + 1.0 * jax.random.uniform(seeds[7], (HEADS,), jnp.float32) ** levels(seeds[7], (HEADS,), ((0, 2),), -0.2, 0.2), 0.5, 1.5)
    pool_codes = scatter_about(part_splits[8], (POOLS, PROWS, STATE), 1.0, 6.0, ((0, 16),))
    pool_scales = jnp.clip(jnp.exp(math.log(0.5) - 2.306499 * jax.random.uniform(part_splits[9], (POOLS, PROWS), jnp.float32) ** levels(part_splits[9], (POOLS, PROWS), ((0, 16),), -0.2, 0.2)), 0.049804688, 0.5).astype(jnp.bfloat16)
    page_holder_keys = jax.random.split(jax.random.fold_in(part_splits[10], 1), N_TP * REQUEST_COUNT * PAGES_TP // (R_DEV * PAGES_TP))
    page_holder_turns = jax.random.permutation(jax.random.fold_in(part_splits[10], 3), N_TP * REQUEST_COUNT * PAGES_TP // (R_DEV * PAGES_TP))
    page_holder = jax.vmap(lambda own, number: routed_block(jax.random.fold_in(part_splits[10], 2), own, number, R_DEV * PAGES_TP, N_REQ, 1, CAP, 2))(page_holder_keys, page_holder_turns).reshape((N_TP, REQUEST_COUNT, PAGES_TP, 1))
    page_index = set_ends(jax.random.randint(part_splits[11], (N_TP, REQUEST_COUNT, PAGES_TP), 0, POOL), jax.random.fold_in(part_splits[11], 1), 0, POOL - 1).astype(jnp.int32)
    hit_blocks = set_ends((jax.random.randint(part_splits[12], (REQUEST_COUNT,), 0, 2) < 1).astype(jnp.int32), jax.random.fold_in(part_splits[12], 1), 0, 1)
    suffix_len = ragged(part_splits[13], REQUEST_COUNT, 3 * REQUEST_COUNT * SUFFIX_SLOTS // 4, SUFFIX_SLOTS, 1).astype(jnp.int32)
    w_out = scatter_about(seeds[14], (INNER, N_TP, D // N_TP), INNER ** -0.5, 0.09375, ((1, 2), (2, 8)))
    return dict(x_inputs=x_inputs, z_gates=z_gates, b_proj=b_proj, c_proj=c_proj, dt_raw=dt_raw, dt_bias=dt_bias, a_log=a_log, d_skip=d_skip, pool_codes=pool_codes, pool_scales=pool_scales, page_holder=page_holder, page_index=page_index, hit_blocks=hit_blocks, suffix_len=suffix_len, w_out=w_out)


def one_request(x_one, z_one, b_one, c_one, raw_one, suffix, hit, page_codes, row_scales, dt_bias, a_log, d_skip, w_flat):
    position = jnp.arange(SUFFIX_SLOTS, dtype=jnp.int32)
    live_mask = (position < suffix).astype(jnp.float32)
    step_size = jax.nn.softplus(raw_one + dt_bias[None, :]) * live_mask[:, None]
    log_decay = -jnp.exp(a_log)[None, :] * jnp.cumsum(step_size, axis=0)
    hit_mask = (hit > 0).astype(jnp.float32)
    start_state = page_codes.astype(jnp.float32) * (row_scales.astype(jnp.float32) * hit_mask)[:, None]
    start_heads = start_state.reshape(HEADS, HD, STATE)
    inner_cb = jnp.dot(c_one, b_one.T, preferred_element_type=jnp.float32)
    causal = position[:, None] >= position[None, :]
    decay_gap = log_decay[:, None, :] - log_decay[None, :, :]
    decay_mat = jnp.exp(jnp.where(causal[:, :, None], decay_gap, -jnp.inf))
    mixer = (decay_mat * inner_cb[:, :, None] * step_size[None, :, :]).astype(jnp.bfloat16)
    x_heads = x_one.reshape(SUFFIX_SLOTS, HEADS, HD).astype(jnp.float32)
    within = jnp.einsum('tsh,shp->thp', mixer.astype(jnp.float32), x_heads)
    from_start = jnp.einsum('tn,hpn->thp', c_one.astype(jnp.float32), start_heads, precision=lax.Precision.HIGHEST)
    y_total = within + jnp.exp(log_decay)[:, :, None] * from_start + d_skip[None, :, None] * x_heads
    gates = z_one.reshape(SUFFIX_SLOTS, HEADS, HD).astype(jnp.float32)
    gated = (y_total * jax.nn.silu(gates) * live_mask[:, None, None]).astype(jnp.bfloat16).reshape(SUFFIX_SLOTS, INNER)
    mixed_out = jnp.dot(gated, w_flat, preferred_element_type=jnp.float32).astype(jnp.bfloat16)
    log_total = log_decay[SUFFIX_SLOTS - 1]
    weight = jnp.exp(log_total[None, :] - log_decay) * step_size
    x_weighted = (x_heads * weight[:, :, None]).astype(jnp.bfloat16)
    accumulated = jnp.einsum('shp,sn->hpn', x_weighted.astype(jnp.float32), b_one.astype(jnp.float32))
    end_state = (jnp.exp(log_total)[:, None, None] * start_heads + accumulated).astype(jnp.bfloat16)
    return mixed_out, end_state.reshape(INNER, STATE)


def reference(x_inputs, z_gates, b_proj, c_proj, dt_raw, dt_bias, a_log, d_skip, pool_codes, pool_scales, page_holder, page_index, hit_blocks, suffix_len, w_out):
    tp_rows = jnp.arange(N_TP, dtype=jnp.int32)[:, None]
    w_flat = w_out.reshape(INNER, D)

    def per_request(request):
        holders = page_holder[:, request, :, 0]
        global_page = ((holders * N_TP + tp_rows) * POOL + page_index[:, request, :]).reshape(-1).astype(jnp.int32)
        page_codes = pool_codes[global_page].reshape(INNER, STATE)
        row_scales = pool_scales[global_page].reshape(INNER)
        return one_request(x_inputs[request], z_gates[request], b_proj[request], c_proj[request], dt_raw[request], suffix_len[request], hit_blocks[request], page_codes, row_scales, dt_bias, a_log, d_skip, w_flat)

    mixed_out, end_state = lax.map(per_request, jnp.arange(REQUEST_COUNT, dtype=jnp.int32))
    return (mixed_out, end_state)
```

```python
import jax
import jax.numpy as jnp
from jax import lax
from jax.sharding import PartitionSpec as P

BF16 = jnp.bfloat16
F32 = jnp.float32


def swapped(value, axis, mask):
    pairs = [(source, source ^ mask) for source in range(lax.axis_size(axis))]
    return lax.ppermute(value, axis, pairs)


def ordered(first_is_mine, mine, other, axis):
    first = jnp.where(first_is_mine, mine, other)
    second = jnp.where(first_is_mine, other, mine)
    return jnp.concatenate([first, second], axis=axis)


def after(value, *earlier):
    return lax.optimization_barrier((value,) + earlier)[0]


def rows_times(tokens, block):
    return lax.dot_general(
        tokens, block, (((1,), (1,)), ((), ())), preferred_element_type=F32
    ).astype(BF16)


def on_device(
    x_inputs,
    z_gates,
    b_proj,
    c_proj,
    dt_raw,
    dt_bias,
    a_log,
    d_skip,
    pool_codes,
    pool_scales,
    page_holder,
    page_index,
    hit_blocks,
    suffix_len,
    w_out,
):
    n_req = lax.axis_size("req")
    own_index = lax.axis_index("req")
    group = lax.axis_index("groups")
    tp_index = lax.axis_index("tp")
    reqs_dev, slots, inner_tp = x_inputs.shape
    heads_tp = dt_raw.shape[2]
    head_dim = inner_tp // heads_tp
    state_width = b_proj.shape[2]
    tokens = reqs_dev * slots

    block = w_out[:, 0, :].T
    columns = block.shape[0]
    share = columns // lax.axis_size("groups")
    piece = lax.dynamic_slice_in_dim(block, group * share, share, 0)
    line = n_req // 2
    chain = line == 4
    if chain:
        near = swapped(piece, "req", 2)
        middle = [(2, 4), (4, 2), (3, 5), (5, 3)]
        outward = [(2, 0), (3, 1), (4, 6), (5, 7)]
        second_inner = lax.ppermute(piece, "req", middle)

    need_count = page_index.shape[2] * reqs_dev
    capacity = max(2, 2 * need_count // n_req)
    holders = page_holder[0, :, :, 0].reshape(n_req, need_count)
    indices = page_index[0].reshape(n_req, need_count)
    is_mine = holders == own_index
    send_rank = jnp.cumsum(is_mine.astype(jnp.int32), axis=1) - 1
    chosen = is_mine[:, None, :] & (
        send_rank[:, None, :] == jnp.arange(capacity, dtype=jnp.int32)[None, :, None]
    )
    wanted = jnp.sum(jnp.where(chosen, indices[:, None, :], 0), axis=2).reshape(-1)
    got_codes = lax.all_to_all(
        pool_codes[wanted], "req", split_axis=0, concat_axis=0, tiled=True
    )
    send_scales = pool_scales[wanted]
    got_scales = lax.all_to_all(send_scales, "req", split_axis=0, concat_axis=0, tiled=True)
    own_holders = lax.dynamic_index_in_dim(holders, own_index, 0, keepdims=False)
    position = jnp.arange(need_count, dtype=jnp.int32)
    earlier = (own_holders[:, None] == own_holders[None, :]) & (
        position[:, None] < position[None, :]
    )
    where_from = own_holders * capacity + jnp.sum(earlier.astype(jnp.int32), axis=0)

    hit_mask = (hit_blocks > 0).astype(F32)
    token_rows = jnp.arange(slots, dtype=jnp.int32)
    live_mask = (token_rows[None, :] < suffix_len[:, None]).astype(F32)
    step_size = jax.nn.softplus(dt_raw + dt_bias) * live_mask[:, :, None]
    log_decay = -jnp.exp(a_log) * jnp.cumsum(step_size, axis=1)
    inner_cb = jnp.einsum("rtn,rsn->rts", c_proj, b_proj, preferred_element_type=F32)
    causal = token_rows[:, None] >= token_rows[None, :]
    decay_gap = log_decay[:, :, None, :] - log_decay[:, None, :, :]
    decay_mat = jnp.exp(jnp.where(causal[None, :, :, None], decay_gap, -jnp.inf))
    mixer = (decay_mat * inner_cb[:, :, :, None] * step_size[:, None, :, :]).astype(BF16)
    x_heads = x_inputs.reshape(reqs_dev, slots, heads_tp, head_dim)
    within = jnp.einsum("rtsh,rshp->rthp", mixer, x_heads, preferred_element_type=F32)
    local = within + d_skip[:, None] * x_heads.astype(F32)
    gates = z_gates.reshape(reqs_dev, slots, heads_tp, head_dim).astype(F32)
    silu = jax.nn.silu(gates) * live_mask[:, :, None, None]
    log_total = log_decay[:, slots - 1, :]
    weight = jnp.exp(log_total[:, None, :] - log_decay) * step_size
    x_weighted = (x_heads.astype(F32) * weight[:, :, :, None]).astype(BF16)
    accumulated = jnp.einsum(
        "rshp,rsn->rhpn", x_weighted, b_proj, preferred_element_type=F32
    )

    page_codes = got_codes[where_from].reshape(reqs_dev, heads_tp, head_dim, state_width)
    row_scales = (
        got_scales[where_from].reshape(reqs_dev, heads_tp, head_dim).astype(F32)
        * hit_mask[:, None, None]
    )
    from_start = jnp.einsum(
        "rtn,rhpn->rthp", c_proj, page_codes, preferred_element_type=F32
    )
    y_total = (
        local + jnp.exp(log_decay)[:, :, :, None] * row_scales[:, None, :, :] * from_start
    )
    gated = (y_total * silu).astype(BF16).reshape(tokens, inner_tp)
    start_state = page_codes.astype(F32) * row_scales[:, :, :, None]
    end_state = (jnp.exp(log_total)[:, :, None, None] * start_state + accumulated).astype(BF16)
    end_state = end_state.reshape(reqs_dev, inner_tp, state_width)

    theirs = swapped(gated, "req", 1)
    own_rows = ordered(tp_index == 0, gated, swapped(gated, "tp", 1), 1)
    their_rows = ordered(tp_index == 0, theirs, swapped(theirs, "tp", 1), 1)

    if chain:
        spot = own_index // 2
        inner = (spot == 1) | (spot == 2)
        low = spot < 2
        second_outer = lax.ppermute(second_inner, "req", outward)
        second = jnp.where(inner, second_inner, second_outer)
        third_inner = lax.ppermute(near, "req", middle)
        third_outer = lax.ppermute(third_inner, "req", outward)
        third = jnp.where(inner, third_inner, third_outer)
        items = [block] + [
            ordered(group == 0, part, swapped(part, "groups", 1), 0)
            for part in (near, second, third)
        ]

        def in_order(parts):
            own, one, two, three = parts
            return (
                jnp.where(spot == 0, own, jnp.where(spot == 1, one, three)),
                jnp.where(spot == 0, one, jnp.where(spot == 1, own, two)),
                jnp.where(spot == 2, own, jnp.where(spot == 3, one, two)),
                jnp.where(spot == 2, one, jnp.where(spot == 3, own, three)),
            )
    else:
        parity = [list(range(first, n_req, 2)) for first in range(2)]
        mine = lax.all_gather(piece, "req", axis=0, axis_index_groups=parity)
        whole = ordered(group == 0, mine, swapped(mine, "groups", 1), 1)
        items = [whole.reshape(line * columns, whole.shape[2])]

        def in_order(parts):
            one = parts[0].reshape(tokens, line, columns)
            return tuple(one[:, at] for at in range(line))

    came = in_order([swapped(rows_times(their_rows, item), "req", 1) for item in items])
    kept = in_order([rows_times(own_rows, item) for item in items])
    even = own_index % 2 == 0
    columns_out = []
    for mine, other in zip(kept, came):
        columns_out += [jnp.where(even, mine, other), jnp.where(even, other, mine)]
    mixed_out = jnp.concatenate(columns_out, axis=1).reshape(reqs_dev, slots, n_req * columns)
    return (mixed_out, end_state)


def solution(mesh):
    in_specs = (
        P(("groups", "req"), None, "tp"),
        P(("groups", "req"), None, "tp"),
        P(("groups", "req"), None, None),
        P(("groups", "req"), None, None),
        P(("groups", "req"), None, "tp"),
        P("tp"),
        P("tp"),
        P("tp"),
        P(("groups", "req", "tp"), None, None),
        P(("groups", "req", "tp"), None),
        P("tp", "groups", None, None),
        P("tp", "groups", None),
        P(("groups", "req")),
        P(("groups", "req")),
        P(None, "tp", "req"),
    )
    out_specs = (P(("groups", "req"), None, "tp"), P(("groups", "req"), "tp", None))
    return jax.shard_map(
        on_device, mesh=mesh, in_specs=in_specs, out_specs=out_specs, check_vma=False
    )
```

```python
import jax
import jax.numpy as jnp
from jax import lax
from jax.experimental import pallas as pl
from jax.experimental.pallas import tpu as pltpu
from jax.sharding import PartitionSpec as P

BF16 = jnp.bfloat16
F32 = jnp.float32


def swapped(value, axis, mask):
    pairs = [(source, source ^ mask) for source in range(lax.axis_size(axis))]
    return lax.ppermute(value, axis, pairs)


NO_COST = pl.CostEstimate(flops=0, bytes_accessed=0, transcendentals=0)
ANYWHERE = pl.BlockSpec(memory_space=pl.ANY)


def after(value, *earlier):
    return lax.optimization_barrier((value,) + earlier)[0]


def held(value, *earlier):
    return pl.pallas_call(
        lambda *refs: None,
        out_shape=jax.ShapeDtypeStruct(value.shape, value.dtype),
        in_specs=[ANYWHERE] * (1 + len(earlier)),
        out_specs=ANYWHERE,
        input_output_aliases={0: 0},
        cost_estimate=NO_COST,
    )(value, *earlier)


def local_kernel(
    heads, skip_ref, x_ref, z_ref, b_ref, c_ref, log_ref, log_rows_ref, step_rows_ref, start_ref, live_ref, *refs
):
    local_ref, factor_ref = refs[-2:]
    slots = x_ref.shape[1]
    width = x_ref.shape[2] // heads
    cb = lax.dot_general(
        c_ref[0], b_ref[0], (((1,), (1,)), ((), ())), preferred_element_type=F32
    )
    later = lax.broadcasted_iota(jnp.int32, (slots, slots), 0)
    causal = later >= lax.broadcasted_iota(jnp.int32, (slots, slots), 1)
    live = live_ref[0]
    for head in range(heads):
        at = slice(head * width, (head + 1) * width)
        gap = log_ref[0, :, head : head + 1] - log_rows_ref[0, head : head + 1, :]
        decay = jnp.exp(jnp.where(causal, gap, -jnp.inf))
        mixer = (decay * cb * step_rows_ref[0, head : head + 1, :]).astype(BF16)
        x = x_ref[0, :, at]
        within = jnp.dot(mixer, x, preferred_element_type=F32)
        z = z_ref[0, :, at].astype(F32)
        silu = z / (1.0 + jnp.exp(-z)) * live
        local_ref[0, :, at] = (within + skip_ref[head] * x.astype(F32)) * silu
        factor_ref[0, :, at] = start_ref[0, :, head : head + 1] * silu


def local_part(d_skip, x_inputs, z_gates, b_proj, c_proj, log_decay, step_size, start_share, live_mask, earlier):
    reqs_dev, slots, inner_tp = x_inputs.shape
    heads = log_decay.shape[2]
    operands = (
        x_inputs,
        z_gates,
        b_proj,
        c_proj,
        log_decay,
        log_decay.transpose(0, 2, 1),
        step_size.transpose(0, 2, 1),
        start_share,
        live_mask[:, :, None],
    )

    def one(array):
        return pl.BlockSpec((1,) + array.shape[1:], lambda request: (request, 0, 0))

    out = jax.ShapeDtypeStruct((reqs_dev, slots, inner_tp), F32)
    return pl.pallas_call(
        lambda *refs: local_kernel(heads, *refs),
        out_shape=[out, out],
        grid=(reqs_dev,),
        in_specs=[pl.BlockSpec(memory_space=pltpu.SMEM)]
        + [one(array) for array in operands]
        + [ANYWHERE] * len(earlier),
        out_specs=[one(out), one(out)],
        compiler_params=pltpu.CompilerParams(vmem_limit_bytes=48 * 2**20),
        cost_estimate=NO_COST,
    )(d_skip, *operands, *earlier)


def state_kernel(heads, where_ref, kept_ref, pages_ref, x_ref, b_ref, weight_ref, out_ref):
    request = pl.program_id(0)
    width = x_ref.shape[2] // heads
    pages = width // pages_ref.shape[1]
    for head in range(heads):
        at = slice(head * width, (head + 1) * width)
        first = (request * heads + head) * pages
        start = jnp.concatenate([pages_ref[where_ref[first + page]] for page in range(pages)], axis=0)
        weighted = (x_ref[0, :, at].astype(F32) * weight_ref[0, :, head : head + 1]).astype(BF16)
        added = lax.dot_general(
            weighted, b_ref[0], (((0,), (0,)), ((), ())), preferred_element_type=F32
        )
        out_ref[0, at, :] = (kept_ref[request, head] * start.astype(F32) + added).astype(BF16)


def state_part(where_from, kept_share, got_pages, x_inputs, b_proj, weight):
    reqs_dev, _, inner_tp = x_inputs.shape
    heads = weight.shape[2]

    def one(array):
        return pl.BlockSpec((1,) + array.shape[1:], lambda request, where_ref, kept_ref: (request, 0, 0))

    out = jax.ShapeDtypeStruct((reqs_dev, inner_tp, b_proj.shape[2]), BF16)
    return pl.pallas_call(
        lambda *refs: state_kernel(heads, *refs),
        out_shape=out,
        grid_spec=pltpu.PrefetchScalarGridSpec(
            num_scalar_prefetch=2,
            grid=(reqs_dev,),
            in_specs=[pl.BlockSpec(memory_space=pltpu.VMEM), one(x_inputs), one(b_proj), one(weight)],
            out_specs=one(out),
        ),
        compiler_params=pltpu.CompilerParams(vmem_limit_bytes=48 * 2**20),
        cost_estimate=NO_COST,
    )(where_from, kept_share, got_pages, x_inputs, b_proj, weight)


def gate_kernel(pages, where_ref, pages_ref, c_ref, local_ref, factor_ref, *refs):
    request, step = pl.program_id(0), pl.program_id(1)
    first = (request * pl.num_programs(1) + step) * pages
    start = jnp.concatenate([pages_ref[where_ref[first + at]] for at in range(pages)], axis=0)
    from_start = lax.dot_general(
        c_ref[0], start, (((1,), (1,)), ((), ())), preferred_element_type=F32
    )
    refs[-1][...] = (local_ref[0] + factor_ref[0] * from_start).astype(BF16)


def gate(where_from, got_pages, c_proj, local, factor, earlier):
    reqs_dev, slots, inner_tp = local.shape
    _, page_rows, state_width = got_pages.shape
    pages = min(8, inner_tp // page_rows)
    wide = pages * page_rows
    steps = inner_tp // wide
    wide_spec = pl.BlockSpec((1, slots, wide), lambda request, step, where_ref: (request, 0, step))

    return pl.pallas_call(
        lambda *refs: gate_kernel(pages, *refs),
        out_shape=jax.ShapeDtypeStruct((reqs_dev * slots, inner_tp), BF16),
        grid_spec=pltpu.PrefetchScalarGridSpec(
            num_scalar_prefetch=1,
            grid=(reqs_dev, steps),
            in_specs=[
                pl.BlockSpec(memory_space=pltpu.VMEM),
                pl.BlockSpec(
                    (1, slots, state_width), lambda request, step, where_ref: (request, 0, 0)
                ),
                wide_spec,
                wide_spec,
            ]
            + [ANYWHERE] * len(earlier),
            out_specs=pl.BlockSpec((slots, wide), lambda request, step, where_ref: (request, step)),
        ),
        compiler_params=pltpu.CompilerParams(vmem_limit_bytes=48 * 2**20),
        cost_estimate=NO_COST,
    )(where_from, got_pages, c_proj, local, factor, *earlier)


def project_kernel(rows, blocks, earlier, place_ref, *refs):
    row_refs, block_refs = refs[: len(rows)], refs[len(rows) : len(rows) + len(blocks)]
    out_ref, held_rows, held_blocks, sems = refs[len(rows) + len(blocks) + earlier :]
    copies = []
    for at, (ref, (first, count, width)) in enumerate(zip(row_refs, rows)):
        lanes = pl.ds(pl.multiple_of(place_ref[at], 128), width)
        copies.append(
            pltpu.make_async_copy(ref, held_rows.at[pl.ds(first, count), lanes], sems.at[at])
        )
    for at, (ref, count) in enumerate(zip(block_refs, blocks), len(rows)):
        first = place_ref[at]
        first = 0 if len(blocks) == 1 else pl.multiple_of(first, 16)
        copies.append(
            pltpu.make_async_copy(ref, held_blocks.at[pl.ds(first, count)], sems.at[at])
        )
    for copy in copies:
        copy.start()
    for copy in copies:
        copy.wait()
    columns = held_blocks.shape[0]
    for first in range(0, columns, 256):
        at = slice(first, min(first + 256, columns))
        out_ref[:, at] = lax.dot_general(
            held_rows[...], held_blocks[at, :], (((1,), (1,)), ((), ())), preferred_element_type=F32
        ).astype(BF16)


def project(rows, blocks, earlier=()):
    count = max(first + array.shape[0] for array, first, _ in rows)
    columns = sum(array.shape[0] for array, _ in blocks)
    inner = blocks[0][0].shape[1]
    place = jnp.stack(
        [jnp.asarray(at, jnp.int32) for _, _, at in rows]
        + [jnp.asarray(at, jnp.int32) for _, at in blocks]
    )
    row_plan = [(first,) + array.shape for array, first, _ in rows]
    block_plan = [array.shape[0] for array, _ in blocks]
    return pl.pallas_call(
        lambda *refs: project_kernel(row_plan, block_plan, len(earlier), *refs),
        out_shape=jax.ShapeDtypeStruct((count, columns), BF16),
        grid_spec=pltpu.PrefetchScalarGridSpec(
            num_scalar_prefetch=1,
            grid=(),
            in_specs=[ANYWHERE] * (len(rows) + len(blocks) + len(earlier)),
            out_specs=pl.BlockSpec(memory_space=pltpu.VMEM),
            scratch_shapes=[
                pltpu.VMEM((count, inner), BF16),
                pltpu.VMEM((columns, inner), BF16),
                pltpu.SemaphoreType.DMA((len(rows) + len(blocks),)),
            ],
        ),
        compiler_params=pltpu.CompilerParams(vmem_limit_bytes=40 * 2**20),
        cost_estimate=NO_COST,
    )(place, *[array for array, _, _ in rows], *[array for array, _ in blocks], *earlier)


def pick_kernel(flag_ref, yes_ref, no_ref, *refs):
    refs[-1][...] = jnp.where(flag_ref[0] == 1, yes_ref[...], no_ref[...])


def pick(flag, yes, no, earlier=()):
    rows, width = yes.shape
    spec = pl.BlockSpec((rows, width), lambda step: (0, 0))
    return pl.pallas_call(
        pick_kernel,
        out_shape=jax.ShapeDtypeStruct(yes.shape, yes.dtype),
        grid=(1,),
        in_specs=[pl.BlockSpec(memory_space=pltpu.SMEM), spec, spec] + [ANYWHERE] * len(earlier),
        out_specs=spec,
        cost_estimate=NO_COST,
    )(flag.astype(jnp.int32).reshape(1), yes, no, *earlier)


def halves_kernel(in_ref, low_ref, high_ref):
    half = low_ref.shape[0]
    low_ref[...] = in_ref[:half]
    high_ref[...] = in_ref[half:]


def halves(array):
    rows, width = array.shape
    out = jax.ShapeDtypeStruct((rows // 2, width), array.dtype)

    def spec(count):
        return pl.BlockSpec((count, width), lambda step: (0, 0))

    return pl.pallas_call(
        halves_kernel,
        out_shape=[out, out],
        grid=(1,),
        in_specs=[spec(rows)],
        out_specs=[spec(rows // 2)] * 2,
        cost_estimate=NO_COST,
    )(array)


def assemble_kernel(place_ref, near_ref, kept_two, kept_three, came_two, came_three, out_ref):
    low, even = place_ref[0] == 1, place_ref[1] == 1
    half = near_ref.shape[1]
    two, three = kept_two[...], kept_three[...]
    kept = (jnp.where(low, two, three), jnp.where(low, three, two))
    two, three = came_two[...], came_three[...]
    came = (jnp.where(low, two, three), jnp.where(low, three, two))
    parts = []
    for mine, other in zip(kept, came):
        parts += [jnp.where(even, mine, other), jnp.where(even, other, mine)]
    far = jnp.concatenate(parts, axis=1)

    @pl.when(low)
    def _():
        out_ref[:, :half] = near_ref[...]
        out_ref[:, half:] = far

    @pl.when(jnp.logical_not(low))
    def _():
        out_ref[:, :half] = far
        out_ref[:, half:] = near_ref[...]


def assemble(low, even, near, kept, came):
    tokens, half = near.shape
    tile = min(128, tokens)

    def spec(width):
        return pl.BlockSpec((tile, width), lambda step, place_ref: (step, 0))

    place = jnp.stack([low.astype(jnp.int32), even.astype(jnp.int32)])
    return pl.pallas_call(
        assemble_kernel,
        out_shape=jax.ShapeDtypeStruct((tokens, 2 * half), BF16),
        grid_spec=pltpu.PrefetchScalarGridSpec(
            num_scalar_prefetch=1,
            grid=(tokens // tile,),
            in_specs=[spec(half)] + [spec(kept[0].shape[1])] * 4,
            out_specs=spec(2 * half),
        ),
        compiler_params=pltpu.CompilerParams(vmem_limit_bytes=16 * 2**20),
        cost_estimate=NO_COST,
    )(place, near, *kept, *came)


def on_device(
    x_inputs,
    z_gates,
    b_proj,
    c_proj,
    dt_raw,
    dt_bias,
    a_log,
    d_skip,
    pool_codes,
    pool_scales,
    page_holder,
    page_index,
    hit_blocks,
    suffix_len,
    w_out,
):
    n_req = lax.axis_size("req")
    own_index = lax.axis_index("req")
    group = lax.axis_index("groups")
    tp_index = lax.axis_index("tp")
    reqs_dev, slots, inner_tp = x_inputs.shape
    tokens = reqs_dev * slots

    latest = []

    def in_turn(value):
        if latest:
            value = after(value, *latest)
        latest[:] = [value]
        return value

    block = w_out[:, 0, :].T
    columns, inner = block.shape
    share = columns // lax.axis_size("groups")
    piece = lax.dynamic_slice_in_dim(block, group * share, share, 0)
    line = n_req // 2
    chain = line == 4
    spot = own_index // 2
    even = own_index % 2 == 0
    low = spot < 2
    inside = (spot == 1) | (spot == 2)
    middle = [(2, 4), (4, 2), (3, 5), (5, 3)]
    outward = [(2, 0), (3, 1), (4, 6), (5, 7)]
    if chain:
        near = swapped(piece, "req", 2)
        second_inner = lax.ppermute(piece, "req", middle)
        beside = swapped(piece, "req", 1)

    need_count = page_index.shape[2] * reqs_dev
    capacity = max(2, 2 * need_count // n_req)
    holders = page_holder[0, :, :, 0].reshape(n_req, need_count)
    indices = page_index[0].reshape(n_req, need_count)
    is_mine = holders == own_index
    send_rank = jnp.cumsum(is_mine.astype(jnp.int32), axis=1) - 1
    chosen = is_mine[:, None, :] & (
        send_rank[:, None, :] == jnp.arange(capacity, dtype=jnp.int32)[None, :, None]
    )
    wanted = jnp.sum(jnp.where(chosen, indices[:, None, :], 0), axis=2).reshape(-1)
    pool = (pool_codes.astype(F32) * pool_scales.astype(F32)[:, :, None]).astype(BF16)
    send_pages = pool[wanted]
    if chain:
        near = in_turn(near)
        second_inner = in_turn(second_inner)
        beside = in_turn(beside)
        near_halves = list(halves(near))
        third_inner = [lax.ppermute(near_halves[0], "req", middle)]
        send_pages = held(send_pages, near, second_inner, beside)
    send_pages = in_turn(send_pages)
    got_pages = lax.all_to_all(send_pages, "req", split_axis=0, concat_axis=0, tiled=True)
    own_holders = lax.dynamic_index_in_dim(holders, own_index, 0, keepdims=False)
    position = jnp.arange(need_count, dtype=jnp.int32)
    earlier = (own_holders[:, None] == own_holders[None, :]) & (
        position[:, None] < position[None, :]
    )
    where_from = own_holders * capacity + jnp.sum(earlier.astype(jnp.int32), axis=0)


    dt_raw = in_turn(dt_raw)
    hit_mask = (hit_blocks > 0).astype(F32)
    token_rows = jnp.arange(slots, dtype=jnp.int32)
    live_mask = (token_rows[None, :] < suffix_len[:, None]).astype(F32)
    step_size = jax.nn.softplus(dt_raw + dt_bias) * live_mask[:, :, None]
    log_decay = -jnp.exp(a_log) * jnp.cumsum(step_size, axis=1)
    start_share = jnp.exp(log_decay) * hit_mask[:, None, None]
    log_total = log_decay[:, slots - 1, :]
    weight = jnp.exp(log_total[:, None, :] - log_decay) * step_size
    kept_share = jnp.exp(log_total) * hit_mask[:, None]
    local, factor = local_part(
        d_skip, x_inputs, z_gates, b_proj, c_proj, log_decay, step_size, start_share, live_mask, [send_pages]
    )

    if chain:
        beside_across = swapped(beside, "groups", 1)
        near_across = swapped(near, "groups", 1)
        near_beside = swapped(near, "req", 1)
        second_outer = lax.ppermute(second_inner, "req", outward)
        local = in_turn(local)
        beside_across = in_turn(beside_across)
        near_across = in_turn(near_across)
        near_beside_across = swapped(near_across, "req", 1)
        near_beside = in_turn(near_beside)
        second_outer = in_turn(second_outer)
        near_beside_across = in_turn(near_beside_across)
        third_inner[0] = in_turn(third_inner[0])
        third_outer = [lax.ppermute(third_inner[0], "req", outward)]
        earlier = [third_inner[0], beside_across, near_beside, near_beside_across, second_outer]
    else:
        earlier = []
    got_pages = in_turn(got_pages)
    gated = in_turn(gate(where_from, got_pages, c_proj, local, factor, earlier))

    first_unit = tp_index * inner_tp
    other_unit = inner_tp - first_unit
    partners = swapped(gated, "tp", 1)
    theirs = swapped(gated, "req", 1)
    if chain:
        third_inner += [lax.ppermute(held(near_halves[1], gated), "req", middle)]
        second = in_turn(pick(inside, second_inner, second_outer, [gated]))
        second_across = swapped(second, "groups", 1)
    partners = in_turn(partners)
    own_rows = [(gated, 0, first_unit), (partners, 0, other_unit)]
    end_state = in_turn(
        state_part(after(where_from, partners), kept_share, got_pages, x_inputs, b_proj, weight)
    )

    if chain:
        spot_bit, parity = spot % 2, own_index % 2
        mine_first, across_first = group * share, (1 - group) * share
        third, third_across = [], []

        def third_part(at):
            part = in_turn(pick(inside, third_inner[at], in_turn(third_outer[at])))
            third.append(part)
            third_across.append(swapped(part, "groups", 1))

        third_inner[1] = in_turn(third_inner[1])
        third_outer += [lax.ppermute(third_inner[1], "req", outward)]
        third_part(0)
        near_blocks = [(block, (spot_bit * 2 + parity) * columns)]
        for bit, odd, mine, across in (
            (spot_bit, 1 - parity, beside, beside_across),
            (1 - spot_bit, parity, near, near_across),
            (1 - spot_bit, 1 - parity, near_beside, near_beside_across),
        ):
            first = (bit * 2 + odd) * columns
            near_blocks += [(mine, first + mine_first), (across, first + across_first)]
        near_out = in_turn(project(own_rows, near_blocks, [third[0]]))
        third_across[0] = in_turn(third_across[0])
        third_part(1)
        second_blocks = [(second, mine_first), (in_turn(second_across), across_first)]
        theirs = in_turn(theirs)
        theirs_other = swapped(theirs, "tp", 1)
        kept = [in_turn(project(own_rows, second_blocks, [third[1], theirs]))]
        theirs_other = in_turn(theirs_other)
        their_rows = [(theirs, 0, first_unit), (theirs_other, 0, other_unit)]
        came = [swapped(in_turn(project(their_rows, second_blocks)), "req", 1)]
        third_across[1] = in_turn(third_across[1])
        third_blocks = []
        for at in range(2):
            half = at * (share // 2)
            third_blocks += [
                (third[at], mine_first + half),
                (third_across[at], across_first + half),
            ]
        came_third = in_turn(project(their_rows, third_blocks))
        came += [swapped(came_third, "req", 1)]
        kept += [project(own_rows, third_blocks, [came_third])]
        mixed_out = assemble(low, even, near_out, kept, came)
    else:
        parities = [list(range(first, n_req, 2)) for first in range(2)]
        mine = lax.all_gather(piece, "req", axis=0, axis_index_groups=parities)
        across = swapped(mine, "groups", 1)
        first_half = jnp.where(group == 0, mine, across)
        second_half = jnp.where(group == 0, across, mine)
        whole = jnp.concatenate([first_half, second_half], axis=1)
        blocks = [(whole.reshape(line * columns, inner), 0)]
        their_rows = [(theirs, 0, first_unit), (swapped(theirs, "tp", 1), 0, other_unit)]
        came = swapped(project(their_rows, blocks), "req", 1).reshape(tokens, line, columns)
        kept = project(own_rows, blocks).reshape(tokens, line, columns)
        both = [jnp.where(even, kept, came), jnp.where(even, came, kept)]
        mixed_out = jnp.stack(both, axis=2)
    mixed_out = mixed_out.reshape(reqs_dev, slots, n_req * columns)
    return (mixed_out, end_state)


def solution(mesh):
    in_specs = (
        P(("groups", "req"), None, "tp"),
        P(("groups", "req"), None, "tp"),
        P(("groups", "req"), None, None),
        P(("groups", "req"), None, None),
        P(("groups", "req"), None, "tp"),
        P("tp"),
        P("tp"),
        P("tp"),
        P(("groups", "req", "tp"), None, None),
        P(("groups", "req", "tp"), None),
        P("tp", "groups", None, None),
        P("tp", "groups", None),
        P(("groups", "req")),
        P(("groups", "req")),
        P(None, "tp", "req"),
    )
    out_specs = (P(("groups", "req"), None, "tp"), P(("groups", "req"), "tp", None))
    return jax.shard_map(
        on_device, mesh=mesh, in_specs=in_specs, out_specs=out_specs, check_vma=False
    )
```

```python
import jax
import jax.numpy as jnp
from jax import lax
from jax.experimental import pallas as pl
from jax.experimental.pallas import tpu as pltpu
from jax.sharding import PartitionSpec as P

BF16 = jnp.bfloat16
F32 = jnp.float32


def swapped(value, axis, mask):
    pairs = [(source, source ^ mask) for source in range(lax.axis_size(axis))]
    return lax.ppermute(value, axis, pairs)


NO_COST = pl.CostEstimate(flops=0, bytes_accessed=0, transcendentals=0)
ANYWHERE = pl.BlockSpec(memory_space=pl.ANY)


def after(value, *earlier):
    return lax.optimization_barrier((value,) + earlier)[0]


def held(value, *earlier):
    return pl.pallas_call(
        lambda *refs: None,
        out_shape=jax.ShapeDtypeStruct(value.shape, value.dtype),
        in_specs=[ANYWHERE] * (1 + len(earlier)),
        out_specs=ANYWHERE,
        input_output_aliases={0: 0},
        cost_estimate=NO_COST,
    )(value, *earlier)


def local_kernel(
    heads, skip_ref, x_ref, z_ref, b_ref, c_ref, log_ref, log_rows_ref, step_rows_ref, start_ref, live_ref, *refs
):
    local_ref, factor_ref = refs[-2:]
    slots = x_ref.shape[1]
    width = x_ref.shape[2] // heads
    cb = lax.dot_general(
        c_ref[0], b_ref[0], (((1,), (1,)), ((), ())), preferred_element_type=F32
    )
    later = lax.broadcasted_iota(jnp.int32, (slots, slots), 0)
    causal = later >= lax.broadcasted_iota(jnp.int32, (slots, slots), 1)
    live = live_ref[0]
    for head in range(heads):
        at = slice(head * width, (head + 1) * width)
        gap = log_ref[0, :, head : head + 1] - log_rows_ref[0, head : head + 1, :]
        decay = jnp.exp(jnp.where(causal, gap, -jnp.inf))
        mixer = (decay * cb * step_rows_ref[0, head : head + 1, :]).astype(BF16)
        x = x_ref[0, :, at]
        within = jnp.dot(mixer, x, preferred_element_type=F32)
        z = z_ref[0, :, at].astype(F32)
        silu = z / (1.0 + jnp.exp(-z)) * live
        local_ref[0, :, at] = (within + skip_ref[head] * x.astype(F32)) * silu
        factor_ref[0, :, at] = start_ref[0, :, head : head + 1] * silu


def local_part(d_skip, x_inputs, z_gates, b_proj, c_proj, log_decay, step_size, start_share, live_mask, earlier):
    reqs_dev, slots, inner_tp = x_inputs.shape
    heads = log_decay.shape[2]
    operands = (
        x_inputs,
        z_gates,
        b_proj,
        c_proj,
        log_decay,
        log_decay.transpose(0, 2, 1),
        step_size.transpose(0, 2, 1),
        start_share,
        live_mask[:, :, None],
    )

    def one(array):
        return pl.BlockSpec((1,) + array.shape[1:], lambda request: (request, 0, 0))

    out = jax.ShapeDtypeStruct((reqs_dev, slots, inner_tp), F32)
    return pl.pallas_call(
        lambda *refs: local_kernel(heads, *refs),
        out_shape=[out, out],
        grid=(reqs_dev,),
        in_specs=[pl.BlockSpec(memory_space=pltpu.SMEM)]
        + [one(array) for array in operands]
        + [ANYWHERE] * len(earlier),
        out_specs=[one(out), one(out)],
        compiler_params=pltpu.CompilerParams(vmem_limit_bytes=48 * 2**20),
        cost_estimate=NO_COST,
    )(d_skip, *operands, *earlier)


def state_kernel(heads, where_ref, kept_ref, pages_ref, x_ref, b_ref, weight_ref, *refs):
    out_ref = refs[-1]
    request = pl.program_id(0)
    width = x_ref.shape[2] // heads
    pages = width // pages_ref.shape[1]
    for head in range(heads):
        at = slice(head * width, (head + 1) * width)
        first = (request * heads + head) * pages
        start = jnp.concatenate([pages_ref[where_ref[first + page]] for page in range(pages)], axis=0)
        weighted = (x_ref[0, :, at].astype(F32) * weight_ref[0, :, head : head + 1]).astype(BF16)
        added = lax.dot_general(
            weighted, b_ref[0], (((0,), (0,)), ((), ())), preferred_element_type=F32
        )
        out_ref[0, at, :] = (kept_ref[request, head] * start.astype(F32) + added).astype(BF16)


def state_part(where_from, kept_share, got_pages, x_inputs, b_proj, weight, earlier):
    reqs_dev, _, inner_tp = x_inputs.shape
    heads = weight.shape[2]

    def one(array):
        return pl.BlockSpec((1,) + array.shape[1:], lambda request, where_ref, kept_ref: (request, 0, 0))

    out = jax.ShapeDtypeStruct((reqs_dev, inner_tp, b_proj.shape[2]), BF16)
    return pl.pallas_call(
        lambda *refs: state_kernel(heads, *refs),
        out_shape=out,
        grid_spec=pltpu.PrefetchScalarGridSpec(
            num_scalar_prefetch=2,
            grid=(reqs_dev,),
            in_specs=[pl.BlockSpec(memory_space=pltpu.VMEM), one(x_inputs), one(b_proj), one(weight)]
            + [ANYWHERE] * len(earlier),
            out_specs=one(out),
        ),
        compiler_params=pltpu.CompilerParams(vmem_limit_bytes=48 * 2**20),
        cost_estimate=NO_COST,
    )(where_from, kept_share, got_pages, x_inputs, b_proj, weight, *earlier)


def gate_kernel(pages, where_ref, pages_ref, c_ref, local_ref, factor_ref, *refs):
    request, step = pl.program_id(0), pl.program_id(1)
    first = (request * pl.num_programs(1) + step) * pages
    start = jnp.concatenate([pages_ref[where_ref[first + at]] for at in range(pages)], axis=0)
    from_start = lax.dot_general(
        c_ref[0], start, (((1,), (1,)), ((), ())), preferred_element_type=F32
    )
    refs[-1][...] = (local_ref[0] + factor_ref[0] * from_start).astype(BF16)


def gate(where_from, got_pages, c_proj, local, factor, earlier):
    reqs_dev, slots, inner_tp = local.shape
    _, page_rows, state_width = got_pages.shape
    pages = min(8, inner_tp // page_rows)
    wide = pages * page_rows
    steps = inner_tp // wide
    wide_spec = pl.BlockSpec((1, slots, wide), lambda request, step, where_ref: (request, 0, step))

    return pl.pallas_call(
        lambda *refs: gate_kernel(pages, *refs),
        out_shape=jax.ShapeDtypeStruct((reqs_dev * slots, inner_tp), BF16),
        grid_spec=pltpu.PrefetchScalarGridSpec(
            num_scalar_prefetch=1,
            grid=(reqs_dev, steps),
            in_specs=[
                pl.BlockSpec(memory_space=pltpu.VMEM),
                pl.BlockSpec(
                    (1, slots, state_width), lambda request, step, where_ref: (request, 0, 0)
                ),
                wide_spec,
                wide_spec,
            ]
            + [ANYWHERE] * len(earlier),
            out_specs=pl.BlockSpec((slots, wide), lambda request, step, where_ref: (request, step)),
        ),
        compiler_params=pltpu.CompilerParams(vmem_limit_bytes=48 * 2**20),
        cost_estimate=NO_COST,
    )(where_from, got_pages, c_proj, local, factor, *earlier)


def project_kernel(rows, blocks, earlier, place_ref, *refs):
    row_refs, block_refs = refs[: len(rows)], refs[len(rows) : len(rows) + len(blocks)]
    out_ref, held_rows, held_blocks, sems = refs[len(rows) + len(blocks) + earlier :]
    copies = []
    for at, (ref, (first, count, width)) in enumerate(zip(row_refs, rows)):
        lanes = pl.ds(pl.multiple_of(place_ref[at], 128), width)
        copies.append(
            pltpu.make_async_copy(ref, held_rows.at[pl.ds(first, count), lanes], sems.at[at])
        )
    for at, (ref, count) in enumerate(zip(block_refs, blocks), len(rows)):
        first = place_ref[at]
        first = 0 if len(blocks) == 1 else pl.multiple_of(first, 16)
        copies.append(
            pltpu.make_async_copy(ref, held_blocks.at[pl.ds(first, count)], sems.at[at])
        )
    for copy in copies:
        copy.start()
    for copy in copies:
        copy.wait()
    columns = held_blocks.shape[0]
    for first in range(0, columns, 256):
        at = slice(first, min(first + 256, columns))
        out_ref[:, at] = lax.dot_general(
            held_rows[...], held_blocks[at, :], (((1,), (1,)), ((), ())), preferred_element_type=F32
        ).astype(BF16)


def project(rows, blocks, earlier=()):
    count = max(first + array.shape[0] for array, first, _ in rows)
    columns = sum(array.shape[0] for array, _ in blocks)
    inner = blocks[0][0].shape[1]
    place = jnp.stack(
        [jnp.asarray(at, jnp.int32) for _, _, at in rows]
        + [jnp.asarray(at, jnp.int32) for _, at in blocks]
    )
    row_plan = [(first,) + array.shape for array, first, _ in rows]
    block_plan = [array.shape[0] for array, _ in blocks]
    return pl.pallas_call(
        lambda *refs: project_kernel(row_plan, block_plan, len(earlier), *refs),
        out_shape=jax.ShapeDtypeStruct((count, columns), BF16),
        grid_spec=pltpu.PrefetchScalarGridSpec(
            num_scalar_prefetch=1,
            grid=(),
            in_specs=[ANYWHERE] * (len(rows) + len(blocks) + len(earlier)),
            out_specs=pl.BlockSpec(memory_space=pltpu.VMEM),
            scratch_shapes=[
                pltpu.VMEM((count, inner), BF16),
                pltpu.VMEM((columns, inner), BF16),
                pltpu.SemaphoreType.DMA((len(rows) + len(blocks),)),
            ],
        ),
        compiler_params=pltpu.CompilerParams(vmem_limit_bytes=60 * 2**20),
        cost_estimate=NO_COST,
    )(place, *[array for array, _, _ in rows], *[array for array, _ in blocks], *earlier)


def pick_kernel(flag_ref, yes_ref, no_ref, *refs):
    refs[-1][...] = jnp.where(flag_ref[0] == 1, yes_ref[...], no_ref[...])


def pick(flag, yes, no, earlier=()):
    rows, width = yes.shape
    spec = pl.BlockSpec((rows, width), lambda step: (0, 0))
    return pl.pallas_call(
        pick_kernel,
        out_shape=jax.ShapeDtypeStruct(yes.shape, yes.dtype),
        grid=(1,),
        in_specs=[pl.BlockSpec(memory_space=pltpu.SMEM), spec, spec] + [ANYWHERE] * len(earlier),
        out_specs=spec,
        cost_estimate=NO_COST,
    )(flag.astype(jnp.int32).reshape(1), yes, no, *earlier)


def halves_kernel(in_ref, low_ref, high_ref):
    half = low_ref.shape[0]
    low_ref[...] = in_ref[:half]
    high_ref[...] = in_ref[half:]


def halves(array):
    rows, width = array.shape
    out = jax.ShapeDtypeStruct((rows // 2, width), array.dtype)

    def spec(count):
        return pl.BlockSpec((count, width), lambda step: (0, 0))

    return pl.pallas_call(
        halves_kernel,
        out_shape=[out, out],
        grid=(1,),
        in_specs=[spec(rows)],
        out_specs=[spec(rows // 2)] * 2,
        cost_estimate=NO_COST,
    )(array)


def assemble_kernel(place_ref, own_ref, kept_ref, two_ref, third_ref, out_ref):
    even = place_ref[0] == 1
    columns = third_ref.shape[1]
    pair = 2 * columns

    def both(mine, other):
        parts = [jnp.where(even, mine, other), jnp.where(even, other, mine)]
        return jnp.concatenate(parts, axis=1)

    pairs = (
        own_ref[:, :pair],
        both(own_ref[:, pair:], two_ref[:, :columns]),
        both(kept_ref[:, :columns], two_ref[:, columns:]),
        both(kept_ref[:, columns:], third_ref[...]),
    )
    for at, value in enumerate(pairs):
        first = pl.multiple_of(place_ref[1 + at], 128)
        out_ref[:, pl.ds(first, pair)] = value


def assemble(spot, even, own, kept, came_two, came_third):
    tokens = own.shape[0]
    columns = came_third.shape[1]
    tile = min(128, tokens)

    def spec(width):
        return pl.BlockSpec((tile, width), lambda step, place_ref: (step, 0))

    low = spot < 2
    order = [spot, spot ^ 1, jnp.where(low, 2, 1), jnp.where(low, 3, 0)]
    place = jnp.stack([even.astype(jnp.int32)] + [(at * 2 * columns).astype(jnp.int32) for at in order])
    return pl.pallas_call(
        assemble_kernel,
        out_shape=jax.ShapeDtypeStruct((tokens, 8 * columns), BF16),
        grid_spec=pltpu.PrefetchScalarGridSpec(
            num_scalar_prefetch=1,
            grid=(tokens // tile,),
            in_specs=[spec(part.shape[1]) for part in (own, kept, came_two, came_third)],
            out_specs=spec(8 * columns),
        ),
        compiler_params=pltpu.CompilerParams(vmem_limit_bytes=16 * 2**20),
        cost_estimate=NO_COST,
    )(place, own, kept, came_two, came_third)


def on_device(
    x_inputs,
    z_gates,
    b_proj,
    c_proj,
    dt_raw,
    dt_bias,
    a_log,
    d_skip,
    pool_codes,
    pool_scales,
    page_holder,
    page_index,
    hit_blocks,
    suffix_len,
    w_out,
):
    n_req = lax.axis_size("req")
    own_index = lax.axis_index("req")
    group = lax.axis_index("groups")
    tp_index = lax.axis_index("tp")
    reqs_dev, slots, inner_tp = x_inputs.shape
    tokens = reqs_dev * slots

    latest = []

    def in_turn(value):
        if latest:
            value = after(value, *latest)
        latest[:] = [value]
        return value

    block = w_out[:, 0, :].T
    columns, inner = block.shape
    share = columns // lax.axis_size("groups")
    piece = lax.dynamic_slice_in_dim(block, group * share, share, 0)
    line = n_req // 2
    chain = line == 4
    spot = own_index // 2
    even = own_index % 2 == 0
    low = spot < 2
    inside = (spot == 1) | (spot == 2)
    middle = [(2, 4), (4, 2), (3, 5), (5, 3)]
    outward = [(2, 0), (3, 1), (4, 6), (5, 7)]
    if chain:
        near = swapped(piece, "req", 2)
        second_inner = lax.ppermute(piece, "req", middle)
        beside = swapped(piece, "req", 1)

    need_count = page_index.shape[2] * reqs_dev
    capacity = max(2, 2 * need_count // n_req)
    holders = page_holder[0, :, :, 0].reshape(n_req, need_count)
    indices = page_index[0].reshape(n_req, need_count)
    is_mine = holders == own_index
    send_rank = jnp.cumsum(is_mine.astype(jnp.int32), axis=1) - 1
    chosen = is_mine[:, None, :] & (
        send_rank[:, None, :] == jnp.arange(capacity, dtype=jnp.int32)[None, :, None]
    )
    wanted = jnp.sum(jnp.where(chosen, indices[:, None, :], 0), axis=2).reshape(-1)
    pool = (pool_codes.astype(F32) * pool_scales.astype(F32)[:, :, None]).astype(BF16)
    send_pages = pool[wanted]
    if chain:
        near = in_turn(near)
        second_inner = in_turn(second_inner)
        beside = in_turn(beside)
        near_halves = list(halves(near))
        third_inner = [lax.ppermute(near_halves[0], "req", middle)]
        send_pages = held(send_pages, near, second_inner, beside)
    send_pages = in_turn(send_pages)
    got_pages = lax.all_to_all(send_pages, "req", split_axis=0, concat_axis=0, tiled=True)
    own_holders = lax.dynamic_index_in_dim(holders, own_index, 0, keepdims=False)
    position = jnp.arange(need_count, dtype=jnp.int32)
    earlier = (own_holders[:, None] == own_holders[None, :]) & (
        position[:, None] < position[None, :]
    )
    where_from = own_holders * capacity + jnp.sum(earlier.astype(jnp.int32), axis=0)


    dt_raw = in_turn(dt_raw)
    hit_mask = (hit_blocks > 0).astype(F32)
    token_rows = jnp.arange(slots, dtype=jnp.int32)
    live_mask = (token_rows[None, :] < suffix_len[:, None]).astype(F32)
    step_size = jax.nn.softplus(dt_raw + dt_bias) * live_mask[:, :, None]
    log_decay = -jnp.exp(a_log) * jnp.cumsum(step_size, axis=1)
    start_share = jnp.exp(log_decay) * hit_mask[:, None, None]
    log_total = log_decay[:, slots - 1, :]
    weight = jnp.exp(log_total[:, None, :] - log_decay) * step_size
    kept_share = jnp.exp(log_total) * hit_mask[:, None]
    local, factor = local_part(
        d_skip, x_inputs, z_gates, b_proj, c_proj, log_decay, step_size, start_share, live_mask, [send_pages]
    )

    if chain:
        beside_across = swapped(beside, "groups", 1)
        near_across = swapped(near, "groups", 1)
        second_outer = lax.ppermute(second_inner, "req", outward)
        local = in_turn(local)
        beside_across = in_turn(beside_across)
        near_across = in_turn(near_across)
        second_outer = in_turn(second_outer)
        second = in_turn(pick(inside, second_inner, second_outer))
        second_across = swapped(second, "groups", 1)
        third_inner[0] = in_turn(third_inner[0])
        third_outer = [lax.ppermute(third_inner[0], "req", outward)]
        earlier = [third_inner[0], beside_across, near_across, second]
    else:
        earlier = []
    got_pages = in_turn(got_pages)
    gated = in_turn(gate(where_from, got_pages, c_proj, local, factor, earlier))

    first_unit = tp_index * inner_tp
    other_unit = inner_tp - first_unit
    partners = swapped(gated, "tp", 1)
    theirs = swapped(gated, "req", 1)
    if chain:
        third_inner += [lax.ppermute(held(near_halves[1], gated), "req", middle)]
    partners = in_turn(partners)
    own_rows = [(gated, 0, first_unit), (partners, 0, other_unit)]

    def state(earlier):
        return in_turn(
            state_part(where_from, kept_share, got_pages, x_inputs, b_proj, weight, earlier)
        )

    if chain:
        mine_first, across_first = group * share, (1 - group) * share

        def halved(mine, across, first):
            return [(mine, first + mine_first), (across, first + across_first)]

        def quartered(mine, across, first):
            quarters = []
            for at in range(2):
                quarters += halved(mine[at], across[at], first + at * (share // 2))
            return quarters

        parity = own_index % 2
        own_blocks = [(block, parity * columns)]
        own_blocks += halved(beside, beside_across, (1 - parity) * columns)
        own_blocks += halved(near, near_across, 2 * columns)
        own_out = in_turn(project(own_rows, own_blocks))
        third, third_across = [], []

        def third_part(at):
            part = in_turn(pick(inside, third_inner[at], in_turn(third_outer[at])))
            third.append(part)
            third_across.append(swapped(part, "groups", 1))

        third_inner[1] = in_turn(third_inner[1])
        third_outer += [lax.ppermute(third_inner[1], "req", outward)]
        third_part(0)
        third_part(1)
        end_state = state([third[1]])
        second_across = in_turn(second_across)
        third_across[0] = in_turn(third_across[0])
        theirs = held(theirs, second_across, third_across[0])
        theirs_other = in_turn(swapped(theirs, "tp", 1))
        their_rows = [(theirs, 0, first_unit), (theirs_other, 0, other_unit)]
        far_blocks = halved(near, near_across, 0) + halved(second, second_across, columns)
        came_two = swapped(in_turn(project(their_rows, far_blocks, [end_state])), "req", 1)
        third_across[1] = in_turn(third_across[1])
        third_blocks = quartered(third, third_across, 0)
        came_third = in_turn(project(their_rows, third_blocks))
        came_two = in_turn(came_two)
        kept = project(
            own_rows,
            halved(second, second_across, 0) + quartered(third, third_across, columns),
            [came_third],
        )
        came_third = swapped(came_third, "req", 1)
        mixed_out = assemble(spot, even, own_out, kept, came_two, came_third)
    else:
        end_state = state([])
        parities = [list(range(first, n_req, 2)) for first in range(2)]
        mine = lax.all_gather(piece, "req", axis=0, axis_index_groups=parities)
        across = swapped(mine, "groups", 1)
        first_half = jnp.where(group == 0, mine, across)
        second_half = jnp.where(group == 0, across, mine)
        whole = jnp.concatenate([first_half, second_half], axis=1)
        blocks = [(whole.reshape(line * columns, inner), 0)]
        their_rows = [(theirs, 0, first_unit), (swapped(theirs, "tp", 1), 0, other_unit)]
        came = swapped(project(their_rows, blocks), "req", 1).reshape(tokens, line, columns)
        kept = project(own_rows, blocks).reshape(tokens, line, columns)
        both = [jnp.where(even, kept, came), jnp.where(even, came, kept)]
        mixed_out = jnp.stack(both, axis=2)
    mixed_out = mixed_out.reshape(reqs_dev, slots, n_req * columns)
    return (mixed_out, end_state)


def solution(mesh):
    in_specs = (
        P(("groups", "req"), None, "tp"),
        P(("groups", "req"), None, "tp"),
        P(("groups", "req"), None, None),
        P(("groups", "req"), None, None),
        P(("groups", "req"), None, "tp"),
        P("tp"),
        P("tp"),
        P("tp"),
        P(("groups", "req", "tp"), None, None),
        P(("groups", "req", "tp"), None),
        P("tp", "groups", None, None),
        P("tp", "groups", None),
        P(("groups", "req")),
        P(("groups", "req")),
        P(None, "tp", "req"),
    )
    out_specs = (P(("groups", "req"), None, "tp"), P(("groups", "req"), "tp", None))
    return jax.shard_map(
        on_device, mesh=mesh, in_specs=in_specs, out_specs=out_specs, check_vma=False
    )
```

```python
import jax
import jax.numpy as jnp
from jax import lax
from jax.experimental import pallas as pl
from jax.experimental.pallas import tpu as pltpu
from jax.sharding import PartitionSpec as P

BF16 = jnp.bfloat16
F32 = jnp.float32


def swapped(value, axis, mask):
    pairs = [(source, source ^ mask) for source in range(lax.axis_size(axis))]
    return lax.ppermute(value, axis, pairs)


NO_COST = pl.CostEstimate(flops=0, bytes_accessed=0, transcendentals=0)
ANYWHERE = pl.BlockSpec(memory_space=pl.ANY)


def after(value, *earlier):
    return lax.optimization_barrier((value,) + earlier)[0]


def held(value, *earlier):
    return pl.pallas_call(
        lambda *refs: None,
        out_shape=jax.ShapeDtypeStruct(value.shape, value.dtype),
        in_specs=[ANYWHERE] * (1 + len(earlier)),
        out_specs=ANYWHERE,
        input_output_aliases={0: 0},
        cost_estimate=NO_COST,
    )(value, *earlier)


def local_kernel(
    heads, skip_ref, x_ref, z_ref, b_ref, c_ref, log_ref, log_rows_ref, step_rows_ref, start_ref, live_ref, *refs
):
    local_ref, factor_ref = refs[-2:]
    slots = x_ref.shape[1]
    width = x_ref.shape[2] // heads
    cb = lax.dot_general(
        c_ref[0], b_ref[0], (((1,), (1,)), ((), ())), preferred_element_type=F32
    )
    later = lax.broadcasted_iota(jnp.int32, (slots, slots), 0)
    causal = later >= lax.broadcasted_iota(jnp.int32, (slots, slots), 1)
    live = live_ref[0]
    for head in range(heads):
        at = slice(head * width, (head + 1) * width)
        gap = log_ref[0, :, head : head + 1] - log_rows_ref[0, head : head + 1, :]
        decay = jnp.exp(jnp.where(causal, gap, -jnp.inf))
        mixer = (decay * cb * step_rows_ref[0, head : head + 1, :]).astype(BF16)
        x = x_ref[0, :, at]
        within = jnp.dot(mixer, x, preferred_element_type=F32)
        z = z_ref[0, :, at].astype(F32)
        silu = z / (1.0 + jnp.exp(-z)) * live
        local_ref[0, :, at] = (within + skip_ref[head] * x.astype(F32)) * silu
        factor_ref[0, :, at] = start_ref[0, :, head : head + 1] * silu


def local_part(d_skip, x_inputs, z_gates, b_proj, c_proj, log_decay, step_size, start_share, live_mask, earlier):
    reqs_dev, slots, inner_tp = x_inputs.shape
    heads = log_decay.shape[2]
    operands = (
        x_inputs,
        z_gates,
        b_proj,
        c_proj,
        log_decay,
        log_decay.transpose(0, 2, 1),
        step_size.transpose(0, 2, 1),
        start_share,
        live_mask[:, :, None],
    )

    def one(array):
        return pl.BlockSpec((1,) + array.shape[1:], lambda request: (request, 0, 0))

    out = jax.ShapeDtypeStruct((reqs_dev, slots, inner_tp), F32)
    return pl.pallas_call(
        lambda *refs: local_kernel(heads, *refs),
        out_shape=[out, out],
        grid=(reqs_dev,),
        in_specs=[pl.BlockSpec(memory_space=pltpu.SMEM)]
        + [one(array) for array in operands]
        + [ANYWHERE] * len(earlier),
        out_specs=[one(out), one(out)],
        compiler_params=pltpu.CompilerParams(vmem_limit_bytes=48 * 2**20),
        cost_estimate=NO_COST,
    )(d_skip, *operands, *earlier)


def state_kernel(heads, where_ref, kept_ref, pages_ref, x_ref, b_ref, weight_ref, *refs):
    out_ref = refs[-1]
    request = pl.program_id(0)
    width = x_ref.shape[2] // heads
    pages = width // pages_ref.shape[1]
    for head in range(heads):
        at = slice(head * width, (head + 1) * width)
        first = (request * heads + head) * pages
        start = jnp.concatenate([pages_ref[where_ref[first + page]] for page in range(pages)], axis=0)
        weighted = (x_ref[0, :, at].astype(F32) * weight_ref[0, :, head : head + 1]).astype(BF16)
        added = lax.dot_general(
            weighted, b_ref[0], (((0,), (0,)), ((), ())), preferred_element_type=F32
        )
        out_ref[0, at, :] = (kept_ref[request, head] * start.astype(F32) + added).astype(BF16)


def state_part(where_from, kept_share, got_pages, x_inputs, b_proj, weight, earlier):
    reqs_dev, _, inner_tp = x_inputs.shape
    heads = weight.shape[2]

    def one(array):
        return pl.BlockSpec((1,) + array.shape[1:], lambda request, where_ref, kept_ref: (request, 0, 0))

    out = jax.ShapeDtypeStruct((reqs_dev, inner_tp, b_proj.shape[2]), BF16)
    return pl.pallas_call(
        lambda *refs: state_kernel(heads, *refs),
        out_shape=out,
        grid_spec=pltpu.PrefetchScalarGridSpec(
            num_scalar_prefetch=2,
            grid=(reqs_dev,),
            in_specs=[pl.BlockSpec(memory_space=pltpu.VMEM), one(x_inputs), one(b_proj), one(weight)]
            + [ANYWHERE] * len(earlier),
            out_specs=one(out),
        ),
        compiler_params=pltpu.CompilerParams(vmem_limit_bytes=60 * 2**20),
        cost_estimate=NO_COST,
    )(where_from, kept_share, got_pages, x_inputs, b_proj, weight, *earlier)


def gate_kernel(pages, where_ref, pages_ref, c_ref, local_ref, factor_ref, *refs):
    request, step = pl.program_id(0), pl.program_id(1)
    first = (request * pl.num_programs(1) + step) * pages
    start = jnp.concatenate([pages_ref[where_ref[first + at]] for at in range(pages)], axis=0)
    from_start = lax.dot_general(
        c_ref[0], start, (((1,), (1,)), ((), ())), preferred_element_type=F32
    )
    refs[-1][...] = (local_ref[0] + factor_ref[0] * from_start).astype(BF16)


def gate(where_from, got_pages, c_proj, local, factor, earlier):
    reqs_dev, slots, inner_tp = local.shape
    _, page_rows, state_width = got_pages.shape
    pages = inner_tp // page_rows
    wide = pages * page_rows
    steps = inner_tp // wide
    wide_spec = pl.BlockSpec((1, slots, wide), lambda request, step, where_ref: (request, 0, step))

    return pl.pallas_call(
        lambda *refs: gate_kernel(pages, *refs),
        out_shape=jax.ShapeDtypeStruct((reqs_dev * slots, inner_tp), BF16),
        grid_spec=pltpu.PrefetchScalarGridSpec(
            num_scalar_prefetch=1,
            grid=(reqs_dev, steps),
            in_specs=[
                pl.BlockSpec(memory_space=pltpu.VMEM),
                pl.BlockSpec(
                    (1, slots, state_width), lambda request, step, where_ref: (request, 0, 0)
                ),
                wide_spec,
                wide_spec,
            ]
            + [ANYWHERE] * len(earlier),
            out_specs=pl.BlockSpec((slots, wide), lambda request, step, where_ref: (request, step)),
        ),
        compiler_params=pltpu.CompilerParams(vmem_limit_bytes=48 * 2**20),
        cost_estimate=NO_COST,
    )(where_from, got_pages, c_proj, local, factor, *earlier)


def project_kernel(rows, blocks, earlier, place_ref, *refs):
    row_refs, block_refs = refs[: len(rows)], refs[len(rows) : len(rows) + len(blocks)]
    out_ref, held_rows, held_blocks, sems = refs[len(rows) + len(blocks) + earlier :]
    copies = []
    for at, (ref, (first, count, width)) in enumerate(zip(row_refs, rows)):
        lanes = pl.ds(pl.multiple_of(place_ref[at], 128), width)
        copies.append(
            pltpu.make_async_copy(ref, held_rows.at[pl.ds(first, count), lanes], sems.at[at])
        )
    for at, (ref, (count, _)) in enumerate(zip(block_refs, blocks), len(rows)):
        first = place_ref[at]
        first = 0 if len(blocks) == 1 else pl.multiple_of(first, 16)
        copies.append(
            pltpu.make_async_copy(ref, held_blocks.at[pl.ds(first, count)], sems.at[at])
        )
    for copy in copies:
        copy.start()
    for copy in copies[: len(rows)]:
        copy.wait()
    columns = held_blocks.shape[0]
    waited = len(rows)
    for first in range(0, columns, 256):
        at = slice(first, min(first + 256, columns))
        while waited < len(copies) and blocks[waited - len(rows)][1] < at.stop:
            copies[waited].wait()
            waited += 1
        out_ref[:, at] = lax.dot_general(
            held_rows[...], held_blocks[at, :], (((1,), (1,)), ((), ())), preferred_element_type=F32
        ).astype(BF16)


def project(rows, blocks, earlier=()):
    count = max(first + array.shape[0] for array, first, _ in rows)
    columns = sum(array.shape[0] for array, _, _ in blocks)
    inner = blocks[0][0].shape[1]
    place = jnp.stack(
        [jnp.asarray(at, jnp.int32) for _, _, at in rows]
        + [jnp.asarray(at, jnp.int32) for _, at, _ in blocks]
    )
    row_plan = [(first,) + array.shape for array, first, _ in rows]
    block_plan = [(array.shape[0], least) for array, _, least in blocks]
    return pl.pallas_call(
        lambda *refs: project_kernel(row_plan, block_plan, len(earlier), *refs),
        out_shape=jax.ShapeDtypeStruct((count, columns), BF16),
        grid_spec=pltpu.PrefetchScalarGridSpec(
            num_scalar_prefetch=1,
            grid=(),
            in_specs=[ANYWHERE] * (len(rows) + len(blocks) + len(earlier)),
            out_specs=pl.BlockSpec(memory_space=pltpu.VMEM),
            scratch_shapes=[
                pltpu.VMEM((count, inner), BF16),
                pltpu.VMEM((columns, inner), BF16),
                pltpu.SemaphoreType.DMA((len(rows) + len(blocks),)),
            ],
        ),
        compiler_params=pltpu.CompilerParams(vmem_limit_bytes=60 * 2**20),
        cost_estimate=NO_COST,
    )(place, *[array for array, _, _ in rows], *[array for array, _, _ in blocks], *earlier)


def pick_kernel(flag_ref, yes_ref, no_ref, *refs):
    refs[-1][...] = jnp.where(flag_ref[0] == 1, yes_ref[...], no_ref[...])


def pick(flag, yes, no, earlier=()):
    rows, width = yes.shape
    spec = pl.BlockSpec((rows, width), lambda step: (0, 0))
    return pl.pallas_call(
        pick_kernel,
        out_shape=jax.ShapeDtypeStruct(yes.shape, yes.dtype),
        grid=(1,),
        in_specs=[pl.BlockSpec(memory_space=pltpu.SMEM), spec, spec] + [ANYWHERE] * len(earlier),
        out_specs=spec,
        cost_estimate=NO_COST,
    )(flag.astype(jnp.int32).reshape(1), yes, no, *earlier)


def halves_kernel(in_ref, low_ref, high_ref):
    half = low_ref.shape[0]
    low_ref[...] = in_ref[:half]
    high_ref[...] = in_ref[half:]


def halves(array):
    rows, width = array.shape
    out = jax.ShapeDtypeStruct((rows // 2, width), array.dtype)

    def spec(count):
        return pl.BlockSpec((count, width), lambda step: (0, 0))

    return pl.pallas_call(
        halves_kernel,
        out_shape=[out, out],
        grid=(1,),
        in_specs=[spec(rows)],
        out_specs=[spec(rows // 2)] * 2,
        cost_estimate=NO_COST,
    )(array)


def assemble_kernel(place_ref, own_ref, kept_second_ref, kept_third_ref, two_ref, third_ref, out_ref):
    even = place_ref[0] == 1
    columns = third_ref.shape[1]
    pair = 2 * columns

    def both(mine, other):
        parts = [jnp.where(even, mine, other), jnp.where(even, other, mine)]
        return jnp.concatenate(parts, axis=1)

    pairs = (
        own_ref[:, :pair],
        both(own_ref[:, pair:], two_ref[:, :columns]),
        both(kept_second_ref[...], two_ref[:, columns:]),
        both(kept_third_ref[...], third_ref[...]),
    )
    for at, value in enumerate(pairs):
        first = pl.multiple_of(place_ref[1 + at], 128)
        out_ref[:, pl.ds(first, pair)] = value


def assemble(spot, even, own, kept, came_two, came_third):
    tokens = own.shape[0]
    columns = came_third.shape[1]
    tile = min(128, tokens)

    def spec(width):
        return pl.BlockSpec((tile, width), lambda step, place_ref: (step, 0))

    low = spot < 2
    order = [spot, spot ^ 1, jnp.where(low, 2, 1), jnp.where(low, 3, 0)]
    place = jnp.stack([even.astype(jnp.int32)] + [(at * 2 * columns).astype(jnp.int32) for at in order])
    return pl.pallas_call(
        assemble_kernel,
        out_shape=jax.ShapeDtypeStruct((tokens, 8 * columns), BF16),
        grid_spec=pltpu.PrefetchScalarGridSpec(
            num_scalar_prefetch=1,
            grid=(tokens // tile,),
            in_specs=[spec(part.shape[1]) for part in (own, *kept, came_two, came_third)],
            out_specs=spec(8 * columns),
        ),
        compiler_params=pltpu.CompilerParams(vmem_limit_bytes=16 * 2**20),
        cost_estimate=NO_COST,
    )(place, own, *kept, came_two, came_third)


def on_device(
    x_inputs,
    z_gates,
    b_proj,
    c_proj,
    dt_raw,
    dt_bias,
    a_log,
    d_skip,
    pool_codes,
    pool_scales,
    page_holder,
    page_index,
    hit_blocks,
    suffix_len,
    w_out,
):
    n_req = lax.axis_size("req")
    own_index = lax.axis_index("req")
    group = lax.axis_index("groups")
    tp_index = lax.axis_index("tp")
    reqs_dev, slots, inner_tp = x_inputs.shape
    tokens = reqs_dev * slots

    latest = []

    def in_turn(value):
        if latest:
            value = after(value, *latest)
        latest[:] = [value]
        return value

    block = w_out[:, 0, :].T
    columns, inner = block.shape
    share = columns // lax.axis_size("groups")
    piece = lax.dynamic_slice_in_dim(block, group * share, share, 0)
    line = n_req // 2
    chain = line == 4
    spot = own_index // 2
    even = own_index % 2 == 0
    low = spot < 2
    inside = (spot == 1) | (spot == 2)
    middle = [(2, 4), (4, 2), (3, 5), (5, 3)]
    outward = [(2, 0), (3, 1), (4, 6), (5, 7)]
    if chain:
        near = swapped(piece, "req", 2)
        second_inner = lax.ppermute(piece, "req", middle)
        beside = swapped(piece, "req", 1)

    need_count = page_index.shape[2] * reqs_dev
    capacity = max(2, 2 * need_count // n_req)
    holders = page_holder[0, :, :, 0].reshape(n_req, need_count)
    indices = page_index[0].reshape(n_req, need_count)
    is_mine = holders == own_index
    send_rank = jnp.cumsum(is_mine.astype(jnp.int32), axis=1) - 1
    chosen = is_mine[:, None, :] & (
        send_rank[:, None, :] == jnp.arange(capacity, dtype=jnp.int32)[None, :, None]
    )
    wanted = jnp.sum(jnp.where(chosen, indices[:, None, :], 0), axis=2).reshape(-1)
    pool = (pool_codes.astype(F32) * pool_scales.astype(F32)[:, :, None]).astype(BF16)
    send_pages = pool[wanted]
    if chain:
        near = in_turn(near)
        second_inner = in_turn(second_inner)
        beside = in_turn(beside)
        near_halves = list(halves(near))
        third_inner = [lax.ppermute(near_halves[0], "req", middle)]
        send_pages = held(send_pages, near, second_inner, beside)
    send_pages = in_turn(send_pages)
    got_pages = lax.all_to_all(send_pages, "req", split_axis=0, concat_axis=0, tiled=True)
    own_holders = lax.dynamic_index_in_dim(holders, own_index, 0, keepdims=False)
    position = jnp.arange(need_count, dtype=jnp.int32)
    earlier = (own_holders[:, None] == own_holders[None, :]) & (
        position[:, None] < position[None, :]
    )
    where_from = own_holders * capacity + jnp.sum(earlier.astype(jnp.int32), axis=0)


    dt_raw = in_turn(dt_raw)
    hit_mask = (hit_blocks > 0).astype(F32)
    token_rows = jnp.arange(slots, dtype=jnp.int32)
    live_mask = (token_rows[None, :] < suffix_len[:, None]).astype(F32)
    step_size = jax.nn.softplus(dt_raw + dt_bias) * live_mask[:, :, None]
    log_decay = -jnp.exp(a_log) * jnp.cumsum(step_size, axis=1)
    start_share = jnp.exp(log_decay) * hit_mask[:, None, None]
    log_total = log_decay[:, slots - 1, :]
    weight = jnp.exp(log_total[:, None, :] - log_decay) * step_size
    kept_share = jnp.exp(log_total) * hit_mask[:, None]
    local, factor = local_part(
        d_skip, x_inputs, z_gates, b_proj, c_proj, log_decay, step_size, start_share, live_mask, [send_pages]
    )

    if chain:
        beside_across = swapped(beside, "groups", 1)
        near_across = swapped(near, "groups", 1)
        second_outer = lax.ppermute(second_inner, "req", outward)
        local = in_turn(local)
        beside_across = in_turn(beside_across)
        near_across = in_turn(near_across)
        second_outer = in_turn(second_outer)
        second = in_turn(pick(inside, second_inner, second_outer))
        second_across = swapped(second, "groups", 1)
        third_inner[0] = in_turn(third_inner[0])
        third_outer = [lax.ppermute(third_inner[0], "req", outward)]
        earlier = [third_inner[0], beside_across, near_across, second]
    else:
        earlier = []
    got_pages = in_turn(got_pages)
    gated = in_turn(gate(where_from, got_pages, c_proj, local, factor, earlier))

    first_unit = tp_index * inner_tp
    other_unit = inner_tp - first_unit
    partners = swapped(gated, "tp", 1)
    theirs = swapped(gated, "req", 1)
    if chain:
        third_inner += [lax.ppermute(held(near_halves[1], gated), "req", middle)]
    partners = in_turn(partners)
    own_rows = [(gated, 0, first_unit), (partners, 0, other_unit)]

    def state(earlier):
        return in_turn(
            state_part(where_from, kept_share, got_pages, x_inputs, b_proj, weight, earlier)
        )

    if chain:
        mine_first, across_first = group * share, (1 - group) * share

        def halved(mine, across, least, more=0):
            return [
                (mine, least + more + mine_first, least),
                (across, least + more + across_first, least),
            ]

        def quartered(mine, across, least):
            quarters = []
            for at in range(2):
                quarters += halved(mine[at], across[at], least, at * (share // 2))
            return quarters

        parity = own_index % 2
        own_blocks = [(block, parity * columns, 0)]
        own_blocks += halved(beside, beside_across, 0, (1 - parity) * columns)
        own_blocks += halved(near, near_across, 2 * columns)
        own_out = in_turn(project(own_rows, own_blocks))
        third, third_across = [], []

        def third_part(at):
            part = in_turn(pick(inside, third_inner[at], in_turn(third_outer[at])))
            third.append(part)
            third_across.append(swapped(part, "groups", 1))

        third_inner[1] = in_turn(third_inner[1])
        third_outer += [lax.ppermute(third_inner[1], "req", outward)]
        third_part(0)
        end_state = state([third[0]])
        third_part(1)
        second_across = in_turn(second_across)
        kept = [in_turn(project(own_rows, halved(second, second_across, 0), [third[1]]))]
        third_across[0] = in_turn(third_across[0])
        theirs = held(theirs, second_across, third_across[0])
        theirs_other = in_turn(swapped(theirs, "tp", 1))
        their_rows = [(theirs, 0, first_unit), (theirs_other, 0, other_unit)]
        far_blocks = halved(near, near_across, 0) + halved(second, second_across, columns)
        came_two = swapped(in_turn(project(their_rows, far_blocks, kept)), "req", 1)
        third_across[1] = in_turn(third_across[1])
        third_blocks = quartered(third, third_across, 0)
        came_third = in_turn(project(their_rows, third_blocks))
        came_two = in_turn(came_two)
        kept += [project(own_rows, third_blocks, [came_third])]
        came_third = swapped(came_third, "req", 1)
        mixed_out = assemble(spot, even, own_out, kept, came_two, came_third)
    else:
        end_state = state([])
        parities = [list(range(first, n_req, 2)) for first in range(2)]
        mine = lax.all_gather(piece, "req", axis=0, axis_index_groups=parities)
        across = swapped(mine, "groups", 1)
        first_half = jnp.where(group == 0, mine, across)
        second_half = jnp.where(group == 0, across, mine)
        whole = jnp.concatenate([first_half, second_half], axis=1)
        blocks = [(whole.reshape(line * columns, inner), 0, 0)]
        their_rows = [(theirs, 0, first_unit), (swapped(theirs, "tp", 1), 0, other_unit)]
        came = swapped(project(their_rows, blocks), "req", 1).reshape(tokens, line, columns)
        kept = project(own_rows, blocks).reshape(tokens, line, columns)
        both = [jnp.where(even, kept, came), jnp.where(even, came, kept)]
        mixed_out = jnp.stack(both, axis=2)
    mixed_out = mixed_out.reshape(reqs_dev, slots, n_req * columns)
    return (mixed_out, end_state)


def solution(mesh):
    in_specs = (
        P(("groups", "req"), None, "tp"),
        P(("groups", "req"), None, "tp"),
        P(("groups", "req"), None, None),
        P(("groups", "req"), None, None),
        P(("groups", "req"), None, "tp"),
        P("tp"),
        P("tp"),
        P("tp"),
        P(("groups", "req", "tp"), None, None),
        P(("groups", "req", "tp"), None),
        P("tp", "groups", None, None),
        P("tp", "groups", None),
        P(("groups", "req")),
        P(("groups", "req")),
        P(None, "tp", "req"),
    )
    out_specs = (P(("groups", "req"), None, "tp"), P(("groups", "req"), "tp", None))
    return jax.shard_map(
        on_device, mesh=mesh, in_specs=in_specs, out_specs=out_specs, check_vma=False
    )
```

```python
import jax
import jax.numpy as jnp
from jax import lax
from jax.experimental import pallas as pl
from jax.experimental.pallas import tpu as pltpu
from jax.sharding import PartitionSpec as P

BF16 = jnp.bfloat16
F32 = jnp.float32


def swapped(value, axis, mask):
    pairs = [(source, source ^ mask) for source in range(lax.axis_size(axis))]
    return lax.ppermute(value, axis, pairs)


NO_COST = pl.CostEstimate(flops=0, bytes_accessed=0, transcendentals=0)
ANYWHERE = pl.BlockSpec(memory_space=pl.ANY)


def after(value, *earlier):
    return lax.optimization_barrier((value,) + earlier)[0]


def held(value, *earlier):
    return pl.pallas_call(
        lambda *refs: None,
        out_shape=jax.ShapeDtypeStruct(value.shape, value.dtype),
        in_specs=[ANYWHERE] * (1 + len(earlier)),
        out_specs=ANYWHERE,
        input_output_aliases={0: 0},
        cost_estimate=NO_COST,
    )(value, *earlier)


def local_kernel(
    heads, skip_ref, x_ref, z_ref, b_ref, c_ref, log_ref, log_rows_ref, step_rows_ref, start_ref, live_ref, *refs
):
    local_ref, factor_ref = refs[-2:]
    slots = x_ref.shape[1]
    width = x_ref.shape[2] // heads
    cb = lax.dot_general(
        c_ref[0], b_ref[0], (((1,), (1,)), ((), ())), preferred_element_type=F32
    )
    later = lax.broadcasted_iota(jnp.int32, (slots, slots), 0)
    causal = later >= lax.broadcasted_iota(jnp.int32, (slots, slots), 1)
    live = live_ref[0]
    for head in range(heads):
        at = slice(head * width, (head + 1) * width)
        gap = log_ref[0, :, head : head + 1] - log_rows_ref[0, head : head + 1, :]
        decay = jnp.exp(jnp.where(causal, gap, -jnp.inf))
        mixer = (decay * cb * step_rows_ref[0, head : head + 1, :]).astype(BF16)
        x = x_ref[0, :, at]
        within = jnp.dot(mixer, x, preferred_element_type=F32)
        z = z_ref[0, :, at].astype(F32)
        silu = z / (1.0 + jnp.exp(-z)) * live
        local_ref[0, :, at] = (within + skip_ref[head] * x.astype(F32)) * silu
        factor_ref[0, :, at] = start_ref[0, :, head : head + 1] * silu


def local_part(d_skip, x_inputs, z_gates, b_proj, c_proj, log_decay, step_size, start_share, live_mask, earlier):
    reqs_dev, slots, inner_tp = x_inputs.shape
    heads = log_decay.shape[2]
    operands = (
        x_inputs,
        z_gates,
        b_proj,
        c_proj,
        log_decay,
        log_decay.transpose(0, 2, 1),
        step_size.transpose(0, 2, 1),
        start_share,
        live_mask[:, :, None],
    )

    def one(array):
        return pl.BlockSpec((1,) + array.shape[1:], lambda request: (request, 0, 0))

    out = jax.ShapeDtypeStruct((reqs_dev, slots, inner_tp), F32)
    return pl.pallas_call(
        lambda *refs: local_kernel(heads, *refs),
        out_shape=[out, out],
        grid=(reqs_dev,),
        in_specs=[pl.BlockSpec(memory_space=pltpu.SMEM)]
        + [one(array) for array in operands]
        + [ANYWHERE] * len(earlier),
        out_specs=[one(out), one(out)],
        compiler_params=pltpu.CompilerParams(vmem_limit_bytes=63 * 2**20),
        cost_estimate=NO_COST,
    )(d_skip, *operands, *earlier)


def state_kernel(heads, where_ref, kept_ref, pages_ref, x_ref, b_ref, weight_ref, *refs):
    out_ref = refs[-1]
    request = pl.program_id(0)
    width = x_ref.shape[2] // heads
    pages = width // pages_ref.shape[1]
    for head in range(heads):
        at = slice(head * width, (head + 1) * width)
        first = (request * heads + head) * pages
        start = jnp.concatenate([pages_ref[where_ref[first + page]] for page in range(pages)], axis=0)
        weighted = (x_ref[0, :, at].astype(F32) * weight_ref[0, :, head : head + 1]).astype(BF16)
        added = lax.dot_general(
            weighted, b_ref[0], (((0,), (0,)), ((), ())), preferred_element_type=F32
        )
        out_ref[0, at, :] = (kept_ref[request, head] * start.astype(F32) + added).astype(BF16)


def state_part(where_from, kept_share, got_pages, x_inputs, b_proj, weight, earlier):
    reqs_dev, _, inner_tp = x_inputs.shape
    heads = weight.shape[2]

    def one(array):
        return pl.BlockSpec((1,) + array.shape[1:], lambda request, where_ref, kept_ref: (request, 0, 0))

    out = jax.ShapeDtypeStruct((reqs_dev, inner_tp, b_proj.shape[2]), BF16)
    return pl.pallas_call(
        lambda *refs: state_kernel(heads, *refs),
        out_shape=out,
        grid_spec=pltpu.PrefetchScalarGridSpec(
            num_scalar_prefetch=2,
            grid=(reqs_dev,),
            in_specs=[pl.BlockSpec(memory_space=pltpu.VMEM), one(x_inputs), one(b_proj), one(weight)]
            + [ANYWHERE] * len(earlier),
            out_specs=one(out),
        ),
        compiler_params=pltpu.CompilerParams(vmem_limit_bytes=63 * 2**20),
        cost_estimate=NO_COST,
    )(where_from, kept_share, got_pages, x_inputs, b_proj, weight, *earlier)


def gate_kernel(pages, where_ref, pages_ref, c_ref, local_ref, factor_ref, *refs):
    request, step = pl.program_id(0), pl.program_id(1)
    first = (request * pl.num_programs(1) + step) * pages
    start = jnp.concatenate([pages_ref[where_ref[first + at]] for at in range(pages)], axis=0)
    from_start = lax.dot_general(
        c_ref[0], start, (((1,), (1,)), ((), ())), preferred_element_type=F32
    )
    refs[-1][...] = (local_ref[0] + factor_ref[0] * from_start).astype(BF16)


def gate(where_from, got_pages, c_proj, local, factor, earlier):
    reqs_dev, slots, inner_tp = local.shape
    _, page_rows, state_width = got_pages.shape
    pages = inner_tp // page_rows
    wide = pages * page_rows
    steps = inner_tp // wide
    wide_spec = pl.BlockSpec((1, slots, wide), lambda request, step, where_ref: (request, 0, step))

    return pl.pallas_call(
        lambda *refs: gate_kernel(pages, *refs),
        out_shape=jax.ShapeDtypeStruct((reqs_dev * slots, inner_tp), BF16),
        grid_spec=pltpu.PrefetchScalarGridSpec(
            num_scalar_prefetch=1,
            grid=(reqs_dev, steps),
            in_specs=[
                pl.BlockSpec(memory_space=pltpu.VMEM),
                pl.BlockSpec(
                    (1, slots, state_width), lambda request, step, where_ref: (request, 0, 0)
                ),
                wide_spec,
                wide_spec,
            ]
            + [ANYWHERE] * len(earlier),
            out_specs=pl.BlockSpec((slots, wide), lambda request, step, where_ref: (request, step)),
        ),
        compiler_params=pltpu.CompilerParams(vmem_limit_bytes=63 * 2**20),
        cost_estimate=NO_COST,
    )(where_from, got_pages, c_proj, local, factor, *earlier)


def project_kernel(rows, blocks, earlier, place_ref, *refs):
    row_refs, block_refs = refs[: len(rows)], refs[len(rows) : len(rows) + len(blocks)]
    out_ref, held_rows, held_blocks, sems = refs[len(rows) + len(blocks) + earlier :]
    copies = []
    for at, (ref, (first, count, width)) in enumerate(zip(row_refs, rows)):
        lanes = pl.ds(pl.multiple_of(place_ref[at], 128), width)
        copies.append(
            pltpu.make_async_copy(ref, held_rows.at[pl.ds(first, count), lanes], sems.at[at])
        )
    for at, (ref, (count, _)) in enumerate(zip(block_refs, blocks), len(rows)):
        first = place_ref[at]
        first = 0 if len(blocks) == 1 else pl.multiple_of(first, 16)
        copies.append(
            pltpu.make_async_copy(ref, held_blocks.at[pl.ds(first, count)], sems.at[at])
        )
    for copy in copies:
        copy.start()
    for copy in copies[: len(rows)]:
        copy.wait()
    columns = held_blocks.shape[0]
    waited = len(rows)
    for first in range(0, columns, 256):
        at = slice(first, min(first + 256, columns))
        while waited < len(copies) and blocks[waited - len(rows)][1] < at.stop:
            copies[waited].wait()
            waited += 1
        out_ref[:, at] = lax.dot_general(
            held_rows[...], held_blocks[at, :], (((1,), (1,)), ((), ())), preferred_element_type=F32
        ).astype(BF16)


def project(rows, blocks, earlier=()):
    count = max(first + array.shape[0] for array, first, _ in rows)
    columns = sum(array.shape[0] for array, _, _ in blocks)
    inner = blocks[0][0].shape[1]
    place = jnp.stack(
        [jnp.asarray(at, jnp.int32) for _, _, at in rows]
        + [jnp.asarray(at, jnp.int32) for _, at, _ in blocks]
    )
    row_plan = [(first,) + array.shape for array, first, _ in rows]
    block_plan = [(array.shape[0], least) for array, _, least in blocks]
    return pl.pallas_call(
        lambda *refs: project_kernel(row_plan, block_plan, len(earlier), *refs),
        out_shape=jax.ShapeDtypeStruct((count, columns), BF16),
        grid_spec=pltpu.PrefetchScalarGridSpec(
            num_scalar_prefetch=1,
            grid=(),
            in_specs=[ANYWHERE] * (len(rows) + len(blocks) + len(earlier)),
            out_specs=pl.BlockSpec(memory_space=pltpu.VMEM),
            scratch_shapes=[
                pltpu.VMEM((count, inner), BF16),
                pltpu.VMEM((columns, inner), BF16),
                pltpu.SemaphoreType.DMA((len(rows) + len(blocks),)),
            ],
        ),
        compiler_params=pltpu.CompilerParams(vmem_limit_bytes=63 * 2**20),
        cost_estimate=NO_COST,
    )(place, *[array for array, _, _ in rows], *[array for array, _, _ in blocks], *earlier)


def pick_kernel(flag_ref, yes_ref, no_ref, *refs):
    refs[-1][...] = jnp.where(flag_ref[0] == 1, yes_ref[...], no_ref[...])


def pick(flag, yes, no, earlier=()):
    rows, width = yes.shape
    spec = pl.BlockSpec((rows, width), lambda step: (0, 0))
    return pl.pallas_call(
        pick_kernel,
        out_shape=jax.ShapeDtypeStruct(yes.shape, yes.dtype),
        grid=(1,),
        in_specs=[pl.BlockSpec(memory_space=pltpu.SMEM), spec, spec] + [ANYWHERE] * len(earlier),
        out_specs=spec,
        cost_estimate=NO_COST,
    )(flag.astype(jnp.int32).reshape(1), yes, no, *earlier)


def halves_kernel(in_ref, low_ref, high_ref):
    half = low_ref.shape[0]
    low_ref[...] = in_ref[:half]
    high_ref[...] = in_ref[half:]


def halves(array):
    rows, width = array.shape
    out = jax.ShapeDtypeStruct((rows // 2, width), array.dtype)

    def spec(count):
        return pl.BlockSpec((count, width), lambda step: (0, 0))

    return pl.pallas_call(
        halves_kernel,
        out_shape=[out, out],
        grid=(1,),
        in_specs=[spec(rows)],
        out_specs=[spec(rows // 2)] * 2,
        cost_estimate=NO_COST,
    )(array)


def assemble_kernel(place_ref, own_ref, kept_second_ref, kept_third_ref, two_ref, third_ref, out_ref):
    even = place_ref[0] == 1
    columns = third_ref.shape[1]
    pair = 2 * columns

    def both(mine, other):
        parts = [jnp.where(even, mine, other), jnp.where(even, other, mine)]
        return jnp.concatenate(parts, axis=1)

    pairs = (
        own_ref[:, :pair],
        both(own_ref[:, pair:], two_ref[:, :columns]),
        both(kept_second_ref[...], two_ref[:, columns:]),
        both(kept_third_ref[...], third_ref[...]),
    )
    for at, value in enumerate(pairs):
        first = pl.multiple_of(place_ref[1 + at], 128)
        out_ref[:, pl.ds(first, pair)] = value


def assemble(spot, even, own, kept, came_two, came_third):
    tokens = own.shape[0]
    columns = came_third.shape[1]
    tile = min(256, tokens)

    def spec(width):
        return pl.BlockSpec((tile, width), lambda step, place_ref: (step, 0))

    low = spot < 2
    order = [spot, spot ^ 1, jnp.where(low, 2, 1), jnp.where(low, 3, 0)]
    place = jnp.stack([even.astype(jnp.int32)] + [(at * 2 * columns).astype(jnp.int32) for at in order])
    return pl.pallas_call(
        assemble_kernel,
        out_shape=jax.ShapeDtypeStruct((tokens, 8 * columns), BF16),
        grid_spec=pltpu.PrefetchScalarGridSpec(
            num_scalar_prefetch=1,
            grid=(tokens // tile,),
            in_specs=[spec(part.shape[1]) for part in (own, *kept, came_two, came_third)],
            out_specs=spec(8 * columns),
        ),
        compiler_params=pltpu.CompilerParams(vmem_limit_bytes=63 * 2**20),
        cost_estimate=NO_COST,
    )(place, own, *kept, came_two, came_third)


def on_device(
    x_inputs,
    z_gates,
    b_proj,
    c_proj,
    dt_raw,
    dt_bias,
    a_log,
    d_skip,
    pool_codes,
    pool_scales,
    page_holder,
    page_index,
    hit_blocks,
    suffix_len,
    w_out,
):
    n_req = lax.axis_size("req")
    own_index = lax.axis_index("req")
    group = lax.axis_index("groups")
    tp_index = lax.axis_index("tp")
    reqs_dev, slots, inner_tp = x_inputs.shape
    tokens = reqs_dev * slots

    latest = []

    def in_turn(value):
        if latest:
            value = after(value, *latest)
        latest[:] = [value]
        return value

    block = w_out[:, 0, :].T
    columns, inner = block.shape
    share = columns // lax.axis_size("groups")
    piece = lax.dynamic_slice_in_dim(block, group * share, share, 0)
    line = n_req // 2
    chain = line == 4
    spot = own_index // 2
    even = own_index % 2 == 0
    low = spot < 2
    inside = (spot == 1) | (spot == 2)
    middle = [(2, 4), (4, 2), (3, 5), (5, 3)]
    outward = [(2, 0), (3, 1), (4, 6), (5, 7)]
    if chain:
        near = swapped(piece, "req", 2)
        second_inner = lax.ppermute(piece, "req", middle)
        beside = swapped(piece, "req", 1)

    need_count = page_index.shape[2] * reqs_dev
    capacity = max(2, 2 * need_count // n_req)
    holders = page_holder[0, :, :, 0].reshape(n_req, need_count)
    indices = page_index[0].reshape(n_req, need_count)
    is_mine = holders == own_index
    send_rank = jnp.cumsum(is_mine.astype(jnp.int32), axis=1) - 1
    chosen = is_mine[:, None, :] & (
        send_rank[:, None, :] == jnp.arange(capacity, dtype=jnp.int32)[None, :, None]
    )
    wanted = jnp.sum(jnp.where(chosen, indices[:, None, :], 0), axis=2).reshape(-1)
    pool = (pool_codes.astype(F32) * pool_scales.astype(F32)[:, :, None]).astype(BF16)
    send_pages = pool[wanted]
    if chain:
        near = in_turn(near)
        second_inner = in_turn(second_inner)
        beside = in_turn(beside)
        near_halves = list(halves(near))
        third_inner = [lax.ppermute(near_halves[0], "req", middle)]
        send_pages = held(send_pages, near, second_inner, beside)
    send_pages = in_turn(send_pages)
    got_pages = lax.all_to_all(send_pages, "req", split_axis=0, concat_axis=0, tiled=True)
    own_holders = lax.dynamic_index_in_dim(holders, own_index, 0, keepdims=False)
    position = jnp.arange(need_count, dtype=jnp.int32)
    earlier = (own_holders[:, None] == own_holders[None, :]) & (
        position[:, None] < position[None, :]
    )
    where_from = own_holders * capacity + jnp.sum(earlier.astype(jnp.int32), axis=0)


    dt_raw = in_turn(dt_raw)
    hit_mask = (hit_blocks > 0).astype(F32)
    token_rows = jnp.arange(slots, dtype=jnp.int32)
    live_mask = (token_rows[None, :] < suffix_len[:, None]).astype(F32)
    step_size = jax.nn.softplus(dt_raw + dt_bias) * live_mask[:, :, None]
    log_decay = -jnp.exp(a_log) * jnp.cumsum(step_size, axis=1)
    start_share = jnp.exp(log_decay) * hit_mask[:, None, None]
    log_total = log_decay[:, slots - 1, :]
    weight = jnp.exp(log_total[:, None, :] - log_decay) * step_size
    kept_share = jnp.exp(log_total) * hit_mask[:, None]
    local, factor = local_part(
        d_skip, x_inputs, z_gates, b_proj, c_proj, log_decay, step_size, start_share, live_mask, [send_pages]
    )

    if chain:
        beside_across = swapped(beside, "groups", 1)
        near_across = swapped(near, "groups", 1)
        second_outer = lax.ppermute(second_inner, "req", outward)
        local = in_turn(local)
        beside_across = in_turn(beside_across)
        near_across = in_turn(near_across)
        second_outer = in_turn(second_outer)
        second = in_turn(pick(inside, second_inner, second_outer))
        second_across = swapped(second, "groups", 1)
        third_inner[0] = in_turn(third_inner[0])
        third_outer = [lax.ppermute(third_inner[0], "req", outward)]
        earlier = [third_inner[0], beside_across, near_across, second]
    else:
        earlier = []
    got_pages = in_turn(got_pages)
    gated = in_turn(gate(where_from, got_pages, c_proj, local, factor, earlier))

    first_unit = tp_index * inner_tp
    other_unit = inner_tp - first_unit
    partners = swapped(gated, "tp", 1)
    theirs = swapped(gated, "req", 1)
    if chain:
        third_inner += [lax.ppermute(held(near_halves[1], gated), "req", middle)]
    partners = in_turn(partners)
    own_rows = [(gated, 0, first_unit), (partners, 0, other_unit)]

    def state(earlier):
        return in_turn(
            state_part(where_from, kept_share, got_pages, x_inputs, b_proj, weight, earlier)
        )

    if chain:
        mine_first, across_first = group * share, (1 - group) * share

        def halved(mine, across, least, more=0):
            return [
                (mine, least + more + mine_first, least),
                (across, least + more + across_first, least),
            ]

        def quartered(mine, across, least):
            quarters = []
            for at in range(2):
                quarters += halved(mine[at], across[at], least, at * (share // 2))
            return quarters

        parity = own_index % 2
        own_blocks = [(block, parity * columns, 0)]
        own_blocks += halved(beside, beside_across, 0, (1 - parity) * columns)
        own_blocks += halved(near, near_across, 2 * columns)
        own_out = in_turn(project(own_rows, own_blocks))
        third, third_across = [], []

        def third_part(at):
            part = in_turn(pick(inside, third_inner[at], in_turn(third_outer[at])))
            third.append(part)
            third_across.append(swapped(part, "groups", 1))

        third_inner[1] = in_turn(third_inner[1])
        third_outer += [lax.ppermute(third_inner[1], "req", outward)]
        third_part(0)
        end_state = state([third[0]])
        third_part(1)
        second_across = in_turn(second_across)
        kept = [in_turn(project(own_rows, halved(second, second_across, 0), [third[1]]))]
        third_across[0] = in_turn(third_across[0])
        theirs = held(theirs, second_across, third_across[0])
        theirs_other = in_turn(swapped(theirs, "tp", 1))
        their_rows = [(theirs, 0, first_unit), (theirs_other, 0, other_unit)]
        far_blocks = halved(near, near_across, 0) + halved(second, second_across, columns)
        came_two = swapped(in_turn(project(their_rows, far_blocks, kept)), "req", 1)
        third_across[1] = in_turn(third_across[1])
        third_blocks = quartered(third, third_across, 0)
        came_third = in_turn(project(their_rows, third_blocks))
        came_two = in_turn(came_two)
        kept += [project(own_rows, third_blocks, [came_third])]
        came_third = swapped(came_third, "req", 1)
        mixed_out = assemble(spot, even, own_out, kept, came_two, came_third)
    else:
        end_state = state([])
        parities = [list(range(first, n_req, 2)) for first in range(2)]
        mine = lax.all_gather(piece, "req", axis=0, axis_index_groups=parities)
        across = swapped(mine, "groups", 1)
        first_half = jnp.where(group == 0, mine, across)
        second_half = jnp.where(group == 0, across, mine)
        whole = jnp.concatenate([first_half, second_half], axis=1)
        blocks = [(whole.reshape(line * columns, inner), 0, 0)]
        their_rows = [(theirs, 0, first_unit), (swapped(theirs, "tp", 1), 0, other_unit)]
        came = swapped(project(their_rows, blocks), "req", 1).reshape(tokens, line, columns)
        kept = project(own_rows, blocks).reshape(tokens, line, columns)
        both = [jnp.where(even, kept, came), jnp.where(even, came, kept)]
        mixed_out = jnp.stack(both, axis=2)
    mixed_out = mixed_out.reshape(reqs_dev, slots, n_req * columns)
    return (mixed_out, end_state)


def solution(mesh):
    in_specs = (
        P(("groups", "req"), None, "tp"),
        P(("groups", "req"), None, "tp"),
        P(("groups", "req"), None, None),
        P(("groups", "req"), None, None),
        P(("groups", "req"), None, "tp"),
        P("tp"),
        P("tp"),
        P("tp"),
        P(("groups", "req", "tp"), None, None),
        P(("groups", "req", "tp"), None),
        P("tp", "groups", None, None),
        P("tp", "groups", None),
        P(("groups", "req")),
        P(("groups", "req")),
        P(None, "tp", "req"),
    )
    out_specs = (P(("groups", "req"), None, "tp"), P(("groups", "req"), "tp", None))
    return jax.shard_map(
        on_device, mesh=mesh, in_specs=in_specs, out_specs=out_specs, check_vma=False
    )
```
